32 devices in a mesh: layer: 4 (over y, x), dp: 8 (over z, core).
Axes of the slice: x: 2, y: 2, z: 4, core: 2. Of those that a mesh axis runs over, the one named last changes fastest.
Arguments:
- activations: bfloat16 [4, 5120, 2048], P('layer', 'dp'), may hold values from -6 to 6
- out_grads: bfloat16 [4, 5120, 512], P('layer', 'dp'), may hold values from -0.059814453 to 0.059814453
- a_inverse: bfloat16 [4, 2048, 2048], P('layer', 'dp'), may hold values from -1 to 3, as said below
- s_inverse: bfloat16 [4, 512, 512], P('layer'), may hold values from -1 to 3, as said below
- in_decay: float32 [4, 2048], P('layer', 'dp'), may hold values from 0 to 1
- out_decay: float32 [4, 512], P('layer'), may hold values from 0 to 1
Outputs:
- direction: bfloat16 [4, 2048, 512], P('layer', 'dp')
The draws below stay inside these ranges and needn't reach their ends.
Inputs may be any that keep to these rules, and one draw needn't show every extreme that they name: `a_inverse`: each layer's matrix is a positive diagonal plus dense small entries. `s_inverse`: each layer's matrix is a positive diagonal plus dense small entries.
All inputs are finite; a program needn't handle non-finite values.
Results may differ from the reference program's by a relative error of at most 0.0036.
Values may be sent and summed in bfloat16 or wider, within the bound.
No kernel may reach another device: no remote copies, remote signals or barrier semaphores. Data moves between devices by JAX's collectives and lax.ppermute only.
A program may use at most 64 MiB of HBM per device.

```python
import math
import jax
import jax.numpy as jnp
from jax import lax

DIN = 2048
DOUT = 512
LAYER_TOTAL = 4
TOKENS = 5120


def dense_inverse(key, order):
    diag_key = jax.random.fold_in(key, 11)
    noise_key = jax.random.fold_in(key, 12)
    diagonal = jax.random.uniform(diag_key, (LAYER_TOTAL, order), jnp.float32, 0.5, 2.0)
    noise = jnp.clip(jax.random.normal(noise_key, (LAYER_TOTAL, order, order), jnp.float32), -5.0, 5.0)
    spread = 0.5 / math.sqrt(order)
    return noise * spread + diagonal[:, :, None] * jnp.eye(order, dtype=jnp.float32)


def draw_a_inverse(key, part):
    return dense_inverse(jax.random.fold_in(key, 101), DIN).astype(jnp.bfloat16)


def draw_s_inverse(key, part):
    return dense_inverse(jax.random.fold_in(key, 202), DOUT).astype(jnp.bfloat16)


def decay_table(key, feature_width):
    flag_key = jax.random.fold_in(key, 21)
    slow_key = jax.random.fold_in(key, 22)
    fast_key = jax.random.fold_in(key, 23)
    jitter_key = jax.random.fold_in(key, 24)
    spike_key = jax.random.fold_in(key, 25)
    level_key = jax.random.fold_in(key, 26)
    share = 0.5
    slow = jax.random.uniform(flag_key, (feature_width,), jnp.float32) < share
    slow_rate = jnp.exp(-jax.random.uniform(slow_key, (feature_width,), jnp.float32) * math.log(10.0) / (2.0 * LAYER_TOTAL))
    fast_rate = jax.random.uniform(fast_key, (feature_width,), jnp.float32, 0.3, 0.6)
    base = jnp.where(slow, slow_rate, fast_rate)
    power = jax.random.uniform(jitter_key, (LAYER_TOTAL, feature_width), jnp.float32, 0.5, 1.5)
    table = base[None, :] ** power
    spike_layers = jax.random.randint(spike_key, (2,), 0, LAYER_TOTAL)
    spike_depth = jax.random.uniform(level_key, (2, feature_width), jnp.float32, 0.5, 0.8)
    layer_numbers = jnp.arange(LAYER_TOTAL)[:, None]
    multiplier = jnp.where(layer_numbers == spike_layers[0], spike_depth[0][None, :], 1.0)
    multiplier = multiplier * jnp.where(layer_numbers == spike_layers[1], spike_depth[1][None, :], 1.0)
    return table * multiplier


def draw_in_decay(key, part):
    return decay_table(jax.random.fold_in(key, 303), DIN)


def draw_out_decay(key, part):
    return decay_table(jax.random.fold_in(key, 404), DOUT)


def block_levels(stream_key, dims, shards, least, top_value):
    def one(axis_at, shards_of):
        steps = jax.random.uniform(jax.random.fold_in(jax.random.fold_in(stream_key, 6), axis_at), (shards_of,), jnp.float32, least / len(shards), top_value / len(shards))
        return jnp.repeat(jnp.exp(steps), dims[axis_at] // shards_of).reshape((-1,) + (1,) * (len(dims) - axis_at - 1))

    loudness = one(*shards[0])
    for cut in shards[1:]:
        loudness = loudness * one(*cut)
    return loudness


def normal_values(rng, dims, scale, bound, split=(), kind=jnp.bfloat16):
    result = jax.random.normal(rng, dims, jnp.float32) * scale
    if len(split) > 0:
        result = block_levels(rng, dims, split, -0.22, 0.18) * result
    return jnp.clip(result, min=-bound, max=bound).astype(kind)


def setup_inputs(seed: int = 0) -> dict:
    key_of = jax.random.split(jax.random.key(seed), 7)
    return {
        "activations": normal_values(key_of[0], (LAYER_TOTAL, TOKENS, DIN), 1.0, 6.0, ((0, 4), (1, 8))),
        "out_grads": normal_values(key_of[1], (LAYER_TOTAL, TOKENS, DOUT), 0.01, 0.059814453, ((0, 4), (1, 8))),
        "a_inverse": draw_a_inverse(jax.random.fold_in(key_of[6], 71), 0),
        "s_inverse": draw_s_inverse(jax.random.fold_in(key_of[6], 71), 0),
        "in_decay": draw_in_decay(jax.random.fold_in(key_of[6], 71), 0),
        "out_decay": draw_out_decay(jax.random.fold_in(key_of[6], 71), 0),
    }


def layer_grad(pair):
    return lax.dot_general(pair[0], pair[1], (((0,), (0,)), ((), ())), preferred_element_type=jnp.float32)

def reference(activations, out_grads, a_inverse, s_inverse, in_decay, out_decay):
    grad = lax.map(layer_grad, (activations, out_grads))
    coupling = in_decay[:, :, None] * out_decay[:, None, :]

    def up_step(carry, pair):
        value = pair[0] + pair[1] * carry
        return (value, value)
    start = jnp.zeros((DIN, DOUT), jnp.float32)
    carry_end, upper = lax.scan(up_step, start, (grad, coupling), reverse=True)

    def side_s(pair):
        return jnp.dot(pair[0].astype(jnp.bfloat16), pair[1], preferred_element_type=jnp.float32).astype(jnp.bfloat16)
    s_applied = lax.map(side_s, (upper, s_inverse))

    def side_a(pair):
        return jnp.dot(pair[0], pair[1], preferred_element_type=jnp.float32)
    solved = lax.map(side_a, (a_inverse, s_applied))

    def down_step(state, pair):
        value = pair[0] + state
        return (pair[1] * value, value)
    state_end, lower = lax.scan(down_step, start, (solved, coupling))
    return lower.astype(jnp.bfloat16)
```

```python
import jax
import jax.numpy as jnp
from jax import lax
from jax.sharding import PartitionSpec as P

MARGIN = 16


def exchange(x, axis, flip):
    return lax.ppermute(x, axis, [(i, i ^ flip) for i in range(lax.axis_size(axis))])


def pack(x):
    top = jnp.maximum(jnp.max(jnp.abs(x)), 1e-30)
    power = jnp.floor(jnp.log2(top))
    body = (x * jnp.exp2(13.0 - power)).astype(jnp.float16)
    tail = jnp.full((MARGIN, x.shape[1]), power.astype(jnp.float16))
    return jnp.concatenate([body, tail], axis=0)


def unpack(message):
    power = message[-1, 0].astype(jnp.float32)
    return message[:-MARGIN].astype(jnp.float32) * jnp.exp2(power - 13.0)


def outer(pair):
    return pair[0][:, None] * pair[1][None, :]


def shards(activations, out_grads, a_inverse, s_inverse, in_decay, out_decay):
    layers, peers = lax.axis_size("layer"), lax.axis_size("dp")
    layer, here = lax.axis_index("layer"), lax.axis_index("dp")
    core, chip = here % 2, here // 2
    rows = a_inverse.shape[1]
    width = out_grads.shape[2]
    tokens = activations.shape[1]
    chips = peers // 2

    rates = (in_decay[0], out_decay[0])
    steps = []
    own = rates
    below = rates
    above = (jnp.ones_like(rates[0]), jnp.ones_like(rates[1]))
    flip = 1
    while flip < layers:
        other = tuple(exchange(r, "layer", flip) for r in own)
        steps.append((flip, own, other, below, above))
        high = (layer & flip) != 0
        above = tuple(jnp.where(high, a * o, a) for a, o in zip(above, other))
        below = tuple(jnp.where(high, b, b * o) for b, o in zip(below, other))
        own = tuple(a * b for a, b in zip(own, other))
        flip *= 2

    window = activations[0].reshape(tokens, chips, 2, rows)
    contract = (((0,), (0,)), ((), ()))

    def partial(of):
        take = lax.dynamic_index_in_dim(window, of, 2, keepdims=False).reshape(tokens, chips * rows)
        return lax.dot_general(take, out_grads[0], contract, preferred_element_type=jnp.float32)

    theirs = unpack(exchange(pack(partial(1 - core)), "dp", 1))
    summed = (partial(core) + theirs).reshape(chips, rows, width)

    def block(at):
        return lax.dynamic_index_in_dim(summed, at, 0, keepdims=False)

    grad = block(chip)
    for flip in range(1, chips):
        grad = grad + unpack(exchange(pack(block(chip ^ flip)), "dp", 2 * flip))

    upper, total = grad, grad
    for flip, mine, other, below, above in steps:
        got = unpack(exchange(pack(total), "layer", flip))
        high = (layer & flip) != 0
        upper = jnp.where(high, upper, upper + outer(below) * got)
        total = jnp.where(high, got + outer(other) * total, total + outer(mine) * got)

    s_applied = jnp.dot(
        upper.astype(jnp.bfloat16), s_inverse[0], preferred_element_type=jnp.float32
    ).astype(jnp.bfloat16)

    parts = [s_applied] + [exchange(s_applied, "dp", 2 * f) for f in range(1, chips)]
    a_rows = a_inverse[0].reshape(rows, chips, 2, rows)
    solved = jnp.zeros((rows, width), jnp.float32)
    for flip, part in enumerate(parts):
        other = exchange(part, "dp", 1)
        for of, operand in ((core, part), (1 - core, other)):
            columns = lax.dynamic_slice(a_rows, (0, chip ^ flip, of, 0), (rows, 1, 1, rows)).reshape(rows, rows)
            solved = solved + jnp.dot(columns, operand, preferred_element_type=jnp.float32)

    lower, total = solved, outer(rates) * solved
    for flip, mine, other, below, above in steps:
        got = unpack(exchange(pack(total), "layer", flip))
        high = (layer & flip) != 0
        lower = jnp.where(high, lower + outer(above) * got, lower)
        total = jnp.where(high, total + outer(mine) * got, got + outer(other) * total)
    return lower.astype(jnp.bfloat16)[None]


def solution(mesh):
    placed = (
        P("layer", "dp", None),
        P("layer", "dp", None),
        P("layer", "dp", None),
        P("layer", None, None),
        P("layer", "dp"),
        P("layer", None),
    )
    return jax.shard_map(
        shards, mesh=mesh, in_specs=placed, out_specs=P("layer", "dp", None), check_vma=False
    )
```

```python
import functools

import jax
import jax.numpy as jnp
from jax import lax
from jax.experimental import pallas as pl
from jax.experimental.pallas import tpu as pltpu
from jax.sharding import PartitionSpec as P

TAIL = 16
LIFT = 2.0**15
TINY = 1e-30
F32, BF16 = jnp.float32, jnp.bfloat16
VMEM = pl.BlockSpec(memory_space=pltpu.VMEM)
SMEM = pl.BlockSpec(memory_space=pltpu.SMEM)


def exchange(x, axis, flip):
    return lax.ppermute(x, axis, [(i, i ^ flip) for i in range(lax.axis_size(axis))])


def put(ref, value):
    rows = value.shape[0]
    top = jnp.max(jnp.max(jnp.abs(value), axis=0, keepdims=True), axis=1, keepdims=True)
    top = jnp.maximum(jnp.broadcast_to(top, (1, value.shape[1])), TINY).astype(BF16).astype(F32)
    ref[rows:, :] = jnp.broadcast_to(top, (TAIL, value.shape[1])).astype(BF16)
    z = value * (LIFT / top)
    z2 = z * z
    z4 = z2 * z2
    z8 = z4 * z4
    ref[:rows, :] = jnp.where(z < 0, -z8, z8).astype(BF16)


def get(ref):
    rows = ref.shape[0] - TAIL
    top = ref[rows:, :][:1, :].astype(F32) * (1.0 / LIFT)
    y = ref[:rows, :].astype(F32)
    square = lax.rsqrt(lax.rsqrt(jnp.abs(y) + 1e-37))
    size = square * lax.rsqrt(square)
    return jnp.where(y < 0, -size, size) * top


def partial_kernel(pick_ref, grads_ref, inputs_ref, out_ref, turned_ref):
    @pl.when(pl.program_id(0) == 0)
    def _():
        turned_ref[...] = grads_ref[0].T

    put(out_ref.at[0], jnp.dot(turned_ref[...], inputs_ref[0], preferred_element_type=F32))


def own_kernel(pick_ref, turned_ref, inputs_ref, out_ref):
    out_ref[0] = jnp.dot(turned_ref[...], inputs_ref[0], preferred_element_type=F32)


def pair_sum_kernel(send, at_ref, own_ref, message_ref, out_ref):
    at = at_ref[0]
    total = own_ref[at] + get(message_ref.at[at])
    if send:
        put(out_ref, total)
    else:
        out_ref[...] = total


def chip_sum_kernel(*refs):
    grad_ref, messages, out_ref, sent_ref = refs[0], refs[1:-2], refs[-2], refs[-1]
    total = grad_ref[...]
    for message in messages:
        total = total + get(message)
    out_ref[...] = total
    put(sent_ref, total)


def step_kernel(value_ref, total_ref, message_ref, a0, a1, b0, b1, c0, c1, value_out, total_out, sent_ref):
    got = get(message_ref)
    value_out[...] = value_ref[...] + (c0[...] * c1[...]) * got
    total = (a0[...] * a1[...]) * total_ref[...] + (b0[...] * b1[...]) * got
    total_out[...] = total
    put(sent_ref, total)


def side_s_kernel(value_ref, message_ref, c0, c1, s_ref, out_ref):
    upper = value_ref[...] + (c0[...] * c1[...]) * get(message_ref)
    out_ref[...] = jnp.dot(s_ref[...], upper.astype(BF16), preferred_element_type=F32).astype(BF16)


def side_a_kernel(*refs):
    at_ref, a_ref, parts = refs[0], refs[1], refs[2:-5]
    r0, r1, solved_ref, total_ref, sent_ref = refs[-5:]
    rows = a_ref.shape[0]
    solved = None
    for i, part in enumerate(parts):
        columns = a_ref[:, pl.ds(pl.multiple_of(at_ref[i] * rows, rows), rows)]
        term = lax.dot_general(part[...], columns, (((1,), (1,)), ((), ())), preferred_element_type=F32)
        solved = term if solved is None else solved + term
    solved_ref[...] = solved
    total = (r0[...] * r1[...]) * solved
    total_ref[...] = total
    put(sent_ref, total)


def last_kernel(value_ref, message_ref, c0, c1, out_ref):
    lower = value_ref[...] + (c0[...] * c1[...]) * get(message_ref)
    out_ref[0] = lower.T.astype(BF16)


def shards(activations, out_grads, a_inverse, s_inverse, in_decay, out_decay):
    layers, peers = lax.axis_size("layer"), lax.axis_size("dp")
    layer, here = lax.axis_index("layer"), lax.axis_index("dp")
    core, chip = here % 2, here // 2
    chips = peers // 2
    rows = a_inverse.shape[1]
    width = out_grads.shape[2]
    tokens = activations.shape[1]
    params = pltpu.CompilerParams(vmem_limit_bytes=32 * 2**20)
    grid_shape = jax.ShapeDtypeStruct((width, rows), F32)
    low_shape = jax.ShapeDtypeStruct((width, rows), BF16)
    sent_shape = jax.ShapeDtypeStruct((width + TAIL, rows), BF16)

    def call(kernel, out_shape, *operands, scalars=0, name=None):
        several = isinstance(out_shape, (list, tuple))
        return pl.pallas_call(
            kernel,
            out_shape=out_shape,
            in_specs=[SMEM] * scalars + [VMEM] * (len(operands) - scalars),
            out_specs=[VMEM] * len(out_shape) if several else VMEM,
            compiler_params=params,
            name=name,
        )(*operands)

    rates = jnp.concatenate([out_decay[0], in_decay[0]])
    ones, zeros = jnp.ones_like(rates), jnp.zeros_like(rates)

    def factors(r):
        return r[:width].reshape(width, 1), r[width:].reshape(1, rows)

    steps = []
    own, below, above = rates, rates, ones
    flip = 1
    while flip < layers:
        other = exchange(own, "layer", flip)
        high = (layer & flip) != 0
        up = (jnp.where(high, other, ones), jnp.where(high, ones, own), jnp.where(high, zeros, below))
        down = (jnp.where(high, ones, other), jnp.where(high, own, ones), jnp.where(high, above, zeros))
        steps.append((flip, [f for r in up for f in factors(r)], [f for r in down for f in factors(r)]))
        above = jnp.where(high, above * other, above)
        below = jnp.where(high, below, below * other)
        own = own * other
        flip *= 2

    def blocks(kernel, of, lead, lead_spec, out_shape, out_specs):
        return pl.pallas_call(
            kernel,
            grid_spec=pltpu.PrefetchScalarGridSpec(
                num_scalar_prefetch=1,
                grid=(chips,),
                in_specs=[lead_spec, pl.BlockSpec((1, tokens, rows), lambda i, pick: (0, 0, 2 * i + pick[0]))],
                out_specs=out_specs,
            ),
            out_shape=out_shape,
            compiler_params=params,
        )(of.reshape(1).astype(jnp.int32), lead, activations)

    message, turned = blocks(
        partial_kernel,
        1 - core,
        out_grads,
        pl.BlockSpec((1, tokens, width), lambda i, pick: (0, 0, 0)),
        [jax.ShapeDtypeStruct((chips, width + TAIL, rows), BF16), jax.ShapeDtypeStruct((width, tokens), BF16)],
        [
            pl.BlockSpec((1, width + TAIL, rows), lambda i, pick: (i, 0, 0)),
            pl.BlockSpec((width, tokens), lambda i, pick: (0, 0)),
        ],
    )
    theirs = exchange(message, "dp", 1)
    mine = blocks(
        own_kernel,
        core,
        turned,
        pl.BlockSpec((width, tokens), lambda i, pick: (0, 0)),
        jax.ShapeDtypeStruct((chips, width, rows), F32),
        pl.BlockSpec((1, width, rows), lambda i, pick: (i, 0, 0)),
    )

    def pair_sum(flip):
        at = (chip ^ flip).reshape(1).astype(jnp.int32)
        kernel = functools.partial(pair_sum_kernel, flip != 0)
        return call(kernel, sent_shape if flip else grid_shape, at, mine, theirs, scalars=1)

    arrived = [exchange(pair_sum(flip), "dp", 2 * flip) for flip in range(1, chips)]
    value, sent = call(chip_sum_kernel, [grid_shape, sent_shape], pair_sum(0), *arrived)

    total = value
    for flip, up, _ in steps[:-1]:
        value, total, sent = call(
            step_kernel, [grid_shape, grid_shape, sent_shape], value, total, exchange(sent, "layer", flip), *up
        )
    flip, up, _ = steps[-1]
    s_applied = call(side_s_kernel, low_shape, value, exchange(sent, "layer", flip), *up[4:], s_inverse[0].T)

    parts, places = [], []
    for flip in range(chips):
        part = exchange(s_applied, "dp", 2 * flip) if flip else s_applied
        parts += [part, exchange(part, "dp", 1)]
        places += [2 * (chip ^ flip) + core, 2 * (chip ^ flip) + 1 - core]
    value, total, sent = call(
        side_a_kernel,
        [grid_shape, grid_shape, sent_shape],
        jnp.stack(places).astype(jnp.int32),
        a_inverse[0],
        *parts,
        *factors(rates),
        scalars=1,
    )

    for flip, _, down in steps[:-1]:
        value, total, sent = call(
            step_kernel, [grid_shape, grid_shape, sent_shape], value, total, exchange(sent, "layer", flip), *down
        )
    flip, _, down = steps[-1]
    return call(
        last_kernel, jax.ShapeDtypeStruct((1, rows, width), BF16), value, exchange(sent, "layer", flip), *down[4:]
    )


def solution(mesh):
    placed = (
        P("layer", "dp", None),
        P("layer", "dp", None),
        P("layer", "dp", None),
        P("layer", None, None),
        P("layer", "dp"),
        P("layer", None),
    )
    return jax.shard_map(
        shards, mesh=mesh, in_specs=placed, out_specs=P("layer", "dp", None), check_vma=False
    )
```

```python
import functools

import jax
import jax.numpy as jnp
from jax import lax
from jax.experimental import pallas as pl
from jax.experimental.pallas import tpu as pltpu
from jax.sharding import PartitionSpec as P

TAIL = 16
LIFT = 2.0**15
TINY = 1e-30
F32, BF16 = jnp.float32, jnp.bfloat16
VMEM = pl.BlockSpec(memory_space=pltpu.VMEM)
SMEM = pl.BlockSpec(memory_space=pltpu.SMEM)
HBM = pl.BlockSpec(memory_space=pltpu.HBM)
FIRST_GRANT = 8
SPLIT = 2


def exchange(x, axis, flip):
    return lax.ppermute(x, axis, [(i, i ^ flip) for i in range(lax.axis_size(axis))])


def put(ref, value):
    rows = value.shape[0]
    top = jnp.max(jnp.max(jnp.abs(value), axis=0, keepdims=True), axis=1, keepdims=True)
    top = jnp.maximum(jnp.broadcast_to(top, (1, value.shape[1])), TINY).astype(BF16).astype(F32)
    ref[rows:, :] = jnp.broadcast_to(top, (TAIL, value.shape[1])).astype(BF16)
    z = value * (LIFT / top)
    z2 = z * z
    z4 = z2 * z2
    z8 = z4 * z4
    ref[:rows, :] = jnp.where(z < 0, -z8, z8).astype(BF16)


def get(ref):
    rows = ref.shape[0] - TAIL
    top = ref[rows:, :][:1, :].astype(F32) * (1.0 / LIFT)
    y = ref[:rows, :].astype(F32)
    square = lax.rsqrt(lax.rsqrt(jnp.abs(y) + 1e-37))
    size = square * lax.rsqrt(square)
    return jnp.where(y < 0, -size, size) * top


def first_kernel(
    core_ref, grads_hbm, inputs_hbm, out_decay, in_decay, out_ref, turned_ref, own_ref, rates_ref, grads_ref, inputs_ref, sems
):
    core = core_ref[0]
    width = out_decay.shape[1]
    rates_ref[:, :width] = out_decay[...]
    rates_ref[:, width:] = in_decay[...]
    chips, _, rows = inputs_ref.shape
    lead = pltpu.make_async_copy(grads_hbm.at[0], grads_ref, sems.at[2 * chips])
    lead.start()

    def load(i, of, into, sem):
        start = pl.multiple_of((2 * i + of) * rows, rows)
        return pltpu.make_async_copy(inputs_hbm.at[0, :, pl.ds(start, rows)], into.at[i], sem)

    theirs = [load(i, 1 - core, inputs_ref, sems.at[i]) for i in range(chips)]
    mine = [load(i, core, own_ref, sems.at[chips + i]) for i in range(chips)]
    for copy in theirs + mine:
        copy.start()
    lead.wait()
    turned_ref[...] = grads_ref[...].T
    for i in range(chips):
        theirs[i].wait()
        put(out_ref.at[i], jnp.dot(turned_ref[...], inputs_ref[i], preferred_element_type=F32))
    for copy in mine:
        copy.wait()


def sum_kernel(part, n, passes, *refs):
    at_ref, turned_ref, own_ref, theirs_ref = refs[:4]
    messages, rest = refs[4 : 4 + n], refs[4 + n :]
    outs = rest[passes:]
    lanes = outs[0].shape[1]
    columns = pl.ds(part * lanes, lanes)
    at = at_ref[0]
    total = jnp.dot(turned_ref[...], own_ref[at, :, columns], preferred_element_type=F32)
    total = total + get(theirs_ref.at[at, :, columns])
    for message in messages:
        total = total + get(message)
    put(outs[0], total)
    if passes:
        for i in range(passes):
            outs[1][i : i + 1, :] = rest[i][...]
    elif len(outs) > 1:
        outs[1][...] = total


def turn_kernel(core_ref, a_ref, s_ref, own_ref, send_ref, s_out):
    core = core_ref[0]
    rows = a_ref.shape[1]
    for i in range(own_ref.shape[0] // rows):
        for of, out in ((core, own_ref), (1 - core, send_ref)):
            columns = pl.ds(pl.multiple_of((2 * i + of) * rows, rows), rows)
            out[i * rows : (i + 1) * rows, :] = a_ref[0, :, columns].T
    s_out[...] = s_ref[0].T


def weight(cols_ref, rows_ref, j):
    return cols_ref[:, j : j + 1] * rows_ref[j : j + 1, :]


def weighed(places, cols_ref, rows_ref, messages, value):
    for j, message in zip(places, messages):
        value = value + weight(cols_ref, rows_ref, j) * get(message)
    return value


def step_kernel(into_value, into_total, more, *refs):
    n = len(into_value)
    value_ref, total_ref, cols_ref, rows_ref = refs[:4]
    messages, outs = refs[4 : 4 + n], refs[4 + n :]
    outs[0][...] = weighed(into_value, cols_ref, rows_ref, messages, value_ref[...])
    total = weight(cols_ref, rows_ref, into_total[0]) * total_ref[...]
    total = weighed(into_total[1:], cols_ref, rows_ref, messages, total)
    put(outs[1], total)
    if more:
        outs[2][...] = total


def cross_kernel(places, part, value_ref, total_ref, cols_ref, rows_ref, message_ref, value_out, sent_ref):
    into_value, mix_own, mix_got = places
    lanes = sent_ref.shape[1]
    columns = slice(part * lanes, (part + 1) * lanes)
    at = rows_ref.at[:, columns]
    got = get(message_ref)
    value_out[...] = value_ref[:, columns] + weight(cols_ref, at, into_value) * got
    put(sent_ref, weight(cols_ref, at, mix_own) * total_ref[:, columns] + weight(cols_ref, at, mix_got) * got)


def side_s_kernel(places, value_ref, s_ref, cols_ref, rows_ref, *refs):
    upper = weighed(places, cols_ref, rows_ref, refs[: len(places)], value_ref[...])
    refs[-1][...] = jnp.dot(s_ref[...], upper.astype(BF16), preferred_element_type=F32).astype(BF16)


def side_a_kernel(n, has_before, start, *refs):
    refs = list(refs)
    at_ref, a_ref = refs.pop(0), refs.pop(0)
    solved = refs.pop(0)[...] if has_before else None
    for i in range(n):
        lanes = refs[i].shape[1]
        features = pl.ds(pl.multiple_of(at_ref[start + i], lanes), lanes)
        term = jnp.dot(refs[i][...], a_ref[features, :], preferred_element_type=F32)
        solved = term if solved is None else solved + term
    if refs[-1].dtype == F32:
        refs[-1][...] = solved
    else:
        put(refs[-1], solved)


def joint_kernel(j, own_ref, theirs_ref, cols_ref, rows_ref, value_ref, total_ref, *sent_refs):
    value = own_ref[...] + get(theirs_ref)
    value_ref[...] = value
    total_ref[...] = weight(cols_ref, rows_ref, j) * value
    for i, sent in enumerate(sent_refs):
        lanes = sent.shape[1]
        put(sent, total_ref[:, i * lanes : (i + 1) * lanes])


def last_kernel(places, *refs):
    cols_ref, rows_ref, out_ref = refs[0], refs[1], refs[-1]
    start, refs = 0, list(refs[2:-1])
    while refs:
        value_ref = refs.pop(0)
        lanes = value_ref.shape[1]
        at = rows_ref.at[:, start : start + lanes]
        lower = weighed(places, cols_ref, at, [refs.pop(0) for _ in places], value_ref[...])
        out_ref[0, start : start + lanes, :] = lower.T.astype(BF16)
        start += lanes


def digits(layers):
    step, out = 1, []
    while step < layers:
        size = min(4, layers // step)
        out.append((step, size))
        step *= size
    return out


def weights_kernel(size, last, n, me_ref, *refs):
    groups, (below_ref, above_ref) = refs[:n], refs[n : n + 2]
    cols_ref, rows_ref, state_ref = refs[n + 2 :]
    group = [ref[i : i + 1, :] for ref in groups for i in range(ref.shape[0])]
    below, above = below_ref[...], above_ref[...]
    me = me_ref[0]
    ones, zeros = jnp.ones_like(below), jnp.zeros_like(below)

    def product(holds):
        out = ones
        for flip, vector in enumerate(group):
            out = out * jnp.where(holds(me ^ flip), vector, ones)
        return out

    def carry(up, source, target):
        if up:
            return jnp.where(source > target, product(lambda q: (q > target) & (q < source)), zeros)
        return jnp.where(source < target, product(lambda q: (q < target) & (q > source)), zeros)

    stack = [group[0]]
    for up, factor in ((True, below), (False, above)):
        if not last:
            stack += [factor * carry(up, me ^ flip, me) for flip in range(1, size)]
            for flip in range(size):
                stack.append(product((lambda q: q < me ^ flip) if up else (lambda q: q > me ^ flip)))
        elif size == 4:
            for first, second in ((1, 2), (2, 1)):
                its, target = me ^ first, me ^ second
                stack += [factor * carry(up, its, me), carry(up, me, target), carry(up, its, target)]
            stack.append(factor)
        else:
            stack.append(factor * carry(up, me ^ 1, me))
    width = cols_ref.shape[0]
    stack += [zeros] * (cols_ref.shape[1] - len(stack))
    table = jnp.concatenate(stack, axis=0)
    cols_ref[...] = table[:, :width].T
    rows_ref[...] = table[: rows_ref.shape[0], width:]
    before = product(lambda q: q < me)
    state_ref[...] = jnp.concatenate([product(lambda q: q >= 0), below * before, above * before], axis=0)


def weight_places(size, last):
    if not last:
        n = 2 * size - 1
        return [(list(range(1 + i * n, i * n + size)), list(range(i * n + size, 1 + i * n + n))) for i in range(2)]
    if size == 4:
        orders = [((1, 2), (0, 1, 2)), ((2, 1), (3, 4, 5))]
        return [([(flips, tuple(1 + 7 * i + j for j in at)) for flips, at in orders], [7 + 7 * i]) for i in range(2)]
    return [(None, [1 + i]) for i in range(2)]


def shards(activations, out_grads, a_inverse, s_inverse, in_decay, out_decay):
    layers, peers = lax.axis_size("layer"), lax.axis_size("dp")
    layer, here = lax.axis_index("layer"), lax.axis_index("dp")
    core, chip = here % 2, here // 2
    chips = peers // 2
    rows = a_inverse.shape[1]
    width = out_grads.shape[2]
    tokens = activations.shape[1]
    split = SPLIT if rows % (128 * SPLIT) == 0 else 1
    lanes = rows // split

    def shape(*dims, dtype=F32):
        return jax.ShapeDtypeStruct(dims, dtype)

    def message(n):
        return shape(width + TAIL, n, dtype=BF16)

    def call(kernel, out_shape, *operands, scalars=0, grant=4 * 2**20, hbm=0, scratch=(), after=()):
        several = isinstance(out_shape, (list, tuple))
        if after:
            inner, count = kernel, len(operands)

            def kernel(*refs):
                inner(*refs[:count], *refs[count + len(after) :])

        return pl.pallas_call(
            kernel,
            out_shape=out_shape,
            in_specs=[SMEM] * scalars
            + [HBM] * hbm
            + [VMEM] * (len(operands) - scalars - hbm)
            + [pl.BlockSpec(memory_space=pl.ANY)] * len(after),
            out_specs=[VMEM] * len(out_shape) if several else VMEM,
            scratch_shapes=scratch,
            compiler_params=pltpu.CompilerParams(vmem_limit_bytes=grant),
            cost_estimate=pl.CostEstimate(flops=10**9, bytes_accessed=10**8, transcendentals=0),
        )(*operands, *after)

    def scalar(x):
        return x.reshape(1).astype(jnp.int32)

    sent, turned, inputs, rates = call(
        first_kernel,
        [
            shape(chips, width + TAIL, rows, dtype=BF16),
            shape(width, tokens, dtype=BF16),
            shape(chips, tokens, rows, dtype=BF16),
            shape(1, width + rows),
        ],
        scalar(core),
        pltpu.with_memory_space_constraint(out_grads, pltpu.HBM),
        pltpu.with_memory_space_constraint(activations, pltpu.HBM),
        out_decay,
        in_decay,
        scalars=1,
        hbm=2,
        grant=FIRST_GRANT * 2**20,
        scratch=[
            pltpu.VMEM((tokens, width), BF16),
            pltpu.VMEM((chips, tokens, rows), BF16),
            pltpu.SemaphoreType.DMA((2 * chips + 1,)),
        ],
    )
    theirs = exchange(sent, "dp", 1)

    levels = [1 << b for b in range(chips.bit_length() - 1)]
    received = [{o: [] for o in range(chips)} for _ in range(split)]
    latest = []

    def block(part, o, *more, passed=(), after=()):
        got = received[part][o]
        outs = call(
            functools.partial(sum_kernel, part, len(got), len(passed)),
            [message(lanes), *more],
            scalar(chip ^ o),
            turned,
            inputs,
            theirs,
            *got,
            *passed,
            scalars=1,
            after=[*latest[-1:], *after],
        )
        latest.append(outs[0])
        return outs

    order = []
    for level in levels:
        sends = list(reversed(range(level, chips, 2 * level)))
        early, late = (sends[:-1], sends[-1:]) if level < levels[-1] else (sends, [])
        order += [(level, o, part) for o in early for part in range(split)]
        order += [(level, o, 0) for o in late]
    order += [(level, level, part) for level in levels[:-1] for part in range(1, split)]

    size = digits(layers)[0][1]
    group = [exchange(rates, "layer", 1)]
    pair_at = min(1, len(order) - 1)
    wait_at = min(3, len(order) - 1)
    for i, (level, o, part) in enumerate(order):
        if i == pair_at:
            sent, pair = block(part, o, shape(2, width + rows), passed=(rates, *group))
            group = [pair] if size < 4 else [pair, exchange(pair, "layer", 2)]
        else:
            [sent] = block(part, o, after=group[1:] if i == wait_at else ())
        received[part][o ^ level].append(exchange(sent, "dp", 2 * level))

    ups, downs = [], []
    below, above = rates, jnp.ones_like(rates)
    for step, size in digits(layers):
        last = step * size == layers
        if step > 1:
            group = [own]
            for bit in (1, 2)[: size.bit_length() - 1]:
                group.append(exchange(jnp.concatenate(group, axis=0), "layer", bit * step))
        cols, in_rows, state = call(
            functools.partial(weights_kernel, size, last, len(group)),
            [shape(width, 128), shape(16, rows), shape(3, width + rows)],
            scalar(layer // step % size),
            *group,
            below,
            above,
            scalars=1,
        )
        own, below, above = state[:1], state[1:2], state[2:]
        for solve, places in zip((ups, downs), weight_places(size, last)):
            solve.append((step, size, cols, in_rows, *places))
    a_own, a_theirs, s_turned = call(
        turn_kernel,
        [shape(chips * rows, rows, dtype=BF16)] * 2 + [shape(width, width, dtype=BF16)],
        scalar(core),
        a_inverse,
        s_inverse,
        scalars=1,
        after=latest[-1:],
    )
    a_theirs = exchange(a_theirs, "dp", 1)

    def steps(solve, value, total, sent, part=0):
        n = value.shape[1]
        for i, (step, size, cols, in_rows, into_value, into_total) in enumerate(solve[:-1]):
            more = i + 1 < len(solve)
            outs = [shape(width, n), message(n)] + [shape(width, n)] * more
            kernel = functools.partial(step_kernel, into_value, into_total, more)
            others = [exchange(sent, "layer", flip * step) for flip in range(1, size)]
            value, sent, total = call(kernel, outs, value, total, cols, in_rows[:, part * n : (part + 1) * n], *others)
        return value, total, sent

    def cross(solve, part, value, total, sent):
        step, size, cols, in_rows, orders, _ = solve[-1]
        n = sent.shape[1]
        if orders is None:
            return value, exchange(sent, "layer", step)
        (first, second), places = orders[part % 2]
        kernel = functools.partial(cross_kernel, places, part if value.shape[1] > n else 0)
        got = exchange(sent, "layer", first * step)
        at = in_rows if value.shape[1] > n or n == rows else in_rows[:, part * n : (part + 1) * n]
        value, sent = call(kernel, [shape(width, n), message(n)], value, total, cols, at, got)
        return value, exchange(sent, "layer", second * step)

    def upper_solve(part, after):
        sent, value = block(part, 0, shape(width, lanes))
        value, total, sent = steps(ups, value, value, sent, part)
        value, got = cross(ups, part, value, total, sent)
        _, _, cols, in_rows, _, places = ups[-1]
        at = in_rows[:, part * lanes : (part + 1) * lanes]
        kernel = functools.partial(side_s_kernel, places)
        return call(kernel, shape(width, lanes, dtype=BF16), value, s_turned, cols, at, got, after=after)

    applied = []
    for part in range(split):
        applied.append(upper_solve(part, applied[-1:]))
    own, others = None, None
    for part in range(split):
        have = {0: applied[part]}
        for level in reversed(levels):
            for o in list(have):
                have[o ^ level] = exchange(have[o], "dp", 2 * level)
        places = jnp.stack([(chip ^ o) * rows + part * lanes for o in have]).astype(jnp.int32)

        def product(a, before, out_shape, after=()):
            before = [] if before is None else [before]
            kernel = functools.partial(side_a_kernel, chips, bool(before), 0)
            return call(kernel, out_shape, places, a, *before, *have.values(), scalars=1, after=after)

        last = part + 1 == split
        others = product(
            a_theirs, others, message(rows) if last else shape(width, rows), [own] if last and own is not None else []
        )
        own = product(a_own, own, shape(width, rows))
    others = exchange(others, "dp", 1)

    pieces = split if len(downs) == 1 and downs[-1][1] == 4 else 1
    outs = [shape(width, rows)] * 2 + [message(rows // pieces)] * pieces
    _, _, cols, in_rows, *_ = downs[0]
    value, total, *sent = call(functools.partial(joint_kernel, 0), outs, own, others, cols, in_rows)
    if pieces == 1:
        value, total, sent[0] = steps(downs, value, total, sent[0])
    operands = [x for part in range(pieces) for x in cross(downs, part, value, total, sent[part])]
    _, _, cols, in_rows, _, places = downs[-1]
    return call(functools.partial(last_kernel, places), shape(1, rows, width, dtype=BF16), cols, in_rows, *operands)


def solution(mesh):
    placed = (
        P("layer", "dp", None),
        P("layer", "dp", None),
        P("layer", "dp", None),
        P("layer", None, None),
        P("layer", "dp"),
        P("layer", None),
    )
    return jax.shard_map(
        shards, mesh=mesh, in_specs=placed, out_specs=P("layer", "dp", None), check_vma=False
    )
```

```python
import functools

import jax
import jax.numpy as jnp
from jax import lax
from jax.experimental import pallas as pl
from jax.experimental.pallas import tpu as pltpu
from jax.sharding import PartitionSpec as P

TAIL = 16
LIFT = 2.0**15
TINY = 1e-30
F32, BF16 = jnp.float32, jnp.bfloat16
VMEM = pl.BlockSpec(memory_space=pltpu.VMEM)
SMEM = pl.BlockSpec(memory_space=pltpu.SMEM)
HBM = pl.BlockSpec(memory_space=pltpu.HBM)
FIRST_GRANT = 8
SPLIT = 2


def exchange(x, axis, flip):
    return lax.ppermute(x, axis, [(i, i ^ flip) for i in range(lax.axis_size(axis))])


def put(ref, value):
    rows = value.shape[0]
    top = jnp.maximum(jnp.max(jnp.abs(value), axis=0, keepdims=True), TINY).astype(BF16).astype(F32)
    ref[rows:, :] = jnp.broadcast_to(top, (TAIL, value.shape[1])).astype(BF16)
    z = value * (LIFT / top)
    z2 = z * z
    z4 = z2 * z2
    z8 = z4 * z4
    ref[:rows, :] = jnp.where(z < 0, -z8, z8).astype(BF16)


def get(ref):
    rows = ref.shape[0] - TAIL
    top = ref[rows:, :][:1, :].astype(F32) * (1.0 / LIFT)
    y = ref[:rows, :].astype(F32)
    square = lax.rsqrt(lax.rsqrt(jnp.abs(y) + 1e-37))
    size = square * lax.rsqrt(square)
    return jnp.where(y < 0, -size, size) * top


def first_kernel(
    here_ref, grads_hbm, inputs_hbm, out_decay, in_decay, sent_ref, turned_ref, rest_ref, own_ref, rates_ref, *scratch
):
    grads_ref, inputs_ref, sems = scratch
    core, chip = here_ref[0], here_ref[1]
    width = out_decay.shape[1]
    chips, _, rows = own_ref.shape
    sem = iter(range(sems.shape[0]))

    def copy(source, into):
        out = pltpu.make_async_copy(source, into, sems.at[next(sem)])
        out.start()
        return out

    def load(o, of, into):
        start = pl.multiple_of((2 * (chip ^ o) + of) * rows, rows)
        return copy(inputs_hbm.at[0, :, pl.ds(start, rows)], into)

    lead = copy(grads_hbm.at[0], grads_ref)
    theirs = [load(o, 1 - core, inputs_ref.at[i]) for i, o in enumerate(range(1, chips, 2))]
    others = [load(o, 1 - core, rest_ref.at[i]) for i, o in enumerate(range(0, chips, 2))]
    others += [load(o, core, own_ref.at[o]) for o in range(chips)]
    others.append(copy(out_decay, rates_ref.at[:, pl.ds(0, width)]))
    others.append(copy(in_decay, rates_ref.at[:, pl.ds(width, rows)]))
    lead.wait()
    turned_ref[...] = grads_ref[...].T
    for i, arrival in enumerate(theirs):
        arrival.wait()
        put(sent_ref.at[i], jnp.dot(turned_ref[...], inputs_ref[i], preferred_element_type=F32))
    for arrival in others:
        arrival.wait()


def rest_kernel(turned_ref, inputs_ref, sent_ref):
    for i in range(inputs_ref.shape[0]):
        put(sent_ref.at[i], jnp.dot(turned_ref[...], inputs_ref[i], preferred_element_type=F32))


def sum_kernel(part, offsets, picks, n, weighs, turned_ref, own_ref, theirs_ref, *refs):
    messages, outs = refs[:n], refs[n + (2 if weighs else 0) :]
    lanes = outs[0].shape[-1]
    columns = pl.ds(part * lanes, lanes)
    for i, o in enumerate(offsets):
        total = jnp.dot(turned_ref[...], own_ref[o, :, columns], preferred_element_type=F32)
        total = total + get(theirs_ref.at[o // 2, :, columns])
        for array, j in picks[i]:
            total = total + get(messages[array].at[j])
        if len(outs) > 1:
            outs[1][...] = total
        if weighs:
            cols_ref, rows_ref = refs[n : n + 2]
            total = weight(cols_ref, rows_ref.at[:, columns], weighs) * total
        put(outs[0].at[i] if len(outs[0].shape) == 3 else outs[0], total)


def turn_kernel(core_ref, a_ref, s_ref, own_ref, send_ref, s_out):
    core = core_ref[0]
    rows = a_ref.shape[1]
    for i in range(own_ref.shape[0] // rows):
        for of, out in ((core, own_ref), (1 - core, send_ref)):
            columns = pl.ds(pl.multiple_of((2 * i + of) * rows, rows), rows)
            out[i * rows : (i + 1) * rows, :] = a_ref[0, :, columns].T
    s_out[...] = s_ref[0].T


def weight(cols_ref, rows_ref, j):
    return cols_ref[:, j : j + 1] * rows_ref[j : j + 1, :]


def weighed(places, cols_ref, rows_ref, messages, value):
    for j, message in zip(places, messages):
        value = value + weight(cols_ref, rows_ref, j) * get(message)
    return value


def step_kernel(into_value, into_total, more, *refs):
    n = len(into_value)
    value_ref, total_ref, cols_ref, rows_ref = refs[:4]
    messages, outs = refs[4 : 4 + n], refs[4 + n :]
    outs[0][...] = weighed(into_value, cols_ref, rows_ref, messages, value_ref[...])
    total = weight(cols_ref, rows_ref, into_total[0]) * total_ref[...]
    total = weighed(into_total[1:], cols_ref, rows_ref, messages, total)
    put(outs[1], total)
    if more:
        outs[2][...] = total


def cross_kernel(places, part, value_ref, total_ref, cols_ref, rows_ref, message_ref, value_out, sent_ref):
    into_value, mix_own, mix_got = places
    lanes = sent_ref.shape[1]
    columns = slice(part * lanes, (part + 1) * lanes)
    at = rows_ref.at[:, columns]
    got = get(message_ref)
    value_out[...] = value_ref[:, columns] + weight(cols_ref, at, into_value) * got
    put(sent_ref, weight(cols_ref, at, mix_own) * total_ref[:, columns] + weight(cols_ref, at, mix_got) * got)


def side_s_kernel(places, value_ref, s_ref, cols_ref, rows_ref, *refs):
    upper = weighed(places, cols_ref, rows_ref, refs[: len(places)], value_ref[...])
    refs[-1][...] = jnp.dot(s_ref[...], upper.astype(BF16), preferred_element_type=F32).astype(BF16)


def stack_kernel(*refs):
    for i, ref in enumerate(refs[:-1]):
        refs[-1][i] = ref[...]


def side_a_kernel(picks, has_before, *refs):
    refs = list(refs)
    at_ref, a_ref = refs.pop(0), refs.pop(0)
    solved = refs.pop(0)[...] if has_before else None
    for array, block, place in picks:
        operand = refs[array][...] if block is None else refs[array][block]
        lanes = operand.shape[1]
        features = pl.ds(pl.multiple_of(at_ref[place], lanes), lanes)
        term = jnp.dot(operand, a_ref[features, :], preferred_element_type=F32)
        solved = term if solved is None else solved + term
    if refs[-1].dtype == F32:
        refs[-1][...] = solved
    else:
        put(refs[-1], solved)


def joint_kernel(total_at, sent_at, own_ref, theirs_ref, cols_ref, rows_ref, value_ref, total_ref, *sent_refs):
    value = own_ref[...] + get(theirs_ref)
    value_ref[...] = value
    total_ref[...] = weight(cols_ref, rows_ref, total_at) * value
    for i, sent in enumerate(sent_refs):
        lanes = sent.shape[1]
        columns = slice(i * lanes, (i + 1) * lanes)
        total = total_ref[:, columns]
        if sent_at[i] is not None:
            total = weight(cols_ref, rows_ref.at[:, columns], sent_at[i]) * total
        put(sent, total)


def last_kernel(places, cols_ref, rows_ref, *refs):
    out_ref = refs[-1]
    for i, place in enumerate(places):
        value_ref, message_ref = refs[2 * i : 2 * i + 2]
        lanes = value_ref.shape[1]
        columns = slice(i * lanes, (i + 1) * lanes)
        lower = weighed([place], cols_ref, rows_ref.at[:, columns], [message_ref], value_ref[...])
        out_ref[0, columns, :] = lower.T.astype(BF16)


def digits(layers):
    step, out = 1, []
    while step < layers:
        size = min(4, layers // step)
        out.append((step, size))
        step *= size
    return out


def weights_kernel(size, last, n, me_ref, *refs):
    groups, (below_ref, above_ref) = refs[:n], refs[n : n + 2]
    cols_ref, rows_ref, *state_ref = refs[n + 2 :]
    group = [ref[i : i + 1, :] for ref in groups for i in range(ref.shape[0])]
    below, above = below_ref[...], above_ref[...]
    ones, zeros = jnp.ones_like(below), jnp.zeros_like(below)

    def product(holds):
        out = ones
        for flip, vector in enumerate(group):
            out = out * jnp.where(holds(me ^ flip), vector, ones)
        return out

    def pick(*cases):
        out = zeros
        for at, vector in cases:
            out = jnp.where(me == at, vector, out)
        return out

    stack = [group[0]]
    for me, factor in ((me_ref[0], below), (size - 1 - me_ref[0], above)):
        if not last:
            for flip in range(1, size):
                peer = me ^ flip
                between = product(lambda q: (q > me) & (q < peer))
                stack.append(jnp.where(peer > me, factor * between, zeros))
            for flip in range(size):
                stack.append(product(lambda q: q < me ^ flip))
        elif size == 4:
            rates, beside = group[:2]
            far = factor * beside
            stack.append(pick((0, factor), (2, factor)))
            stack.append(pick((2, ones), (3, beside)))
            stack.append(pick((2, rates), (3, ones)))
            stack.append(pick((0, far), (1, factor)))
            stack.append(pick((0, far), (1, factor)))
            stack.append(pick((1, ones), (3, ones)))
            stack.append(pick((0, ones), (1, rates)))
            stack.append(pick((0, factor), (1, factor), (2, factor)))
            stack.append(pick((0, ones), (1, ones), (2, ones), (3, beside)))
        else:
            stack.append(pick((0, factor)))
    width = cols_ref.shape[0]
    stack += [zeros] * (cols_ref.shape[1] - len(stack))
    table = jnp.concatenate(stack, axis=0)
    cols_ref[...] = table[:, :width].T
    rows_ref[...] = table[: rows_ref.shape[0], width:]
    if not last:
        me = me_ref[0]
        before = product(lambda q: q < me)
        state_ref[0][...] = jnp.concatenate([product(lambda q: q >= 0), below * before, above * before], axis=0)


def weight_places(size, last):
    out = []
    for i in range(2):
        if not last:
            n = 2 * size - 1
            out.append((list(range(1 + i * n, i * n + size)), list(range(i * n + size, 1 + i * n + n))))
        elif size == 4:
            b = 1 + 9 * i
            out.append(([((1, 2), None, (b, b + 1, b + 2), b + 3), ((2, 1), b + 8, (b + 4, b + 5, b + 6), b + 7)], None))
        else:
            out.append((None, 1 + i))
    return out


def shards(activations, out_grads, a_inverse, s_inverse, in_decay, out_decay):
    layers, peers = lax.axis_size("layer"), lax.axis_size("dp")
    layer, here = lax.axis_index("layer"), lax.axis_index("dp")
    core, chip = here % 2, here // 2
    chips = peers // 2
    rows = a_inverse.shape[1]
    width = out_grads.shape[2]
    tokens = activations.shape[1]
    split = SPLIT if rows % (128 * SPLIT) == 0 else 1
    lanes = rows // split

    def shape(*dims, dtype=F32):
        return jax.ShapeDtypeStruct(dims, dtype)

    def message(n):
        return shape(width + TAIL, n, dtype=BF16)

    def call(kernel, out_shape, *operands, scalars=0, grant=4 * 2**20, hbm=0, scratch=(), after=()):
        several = isinstance(out_shape, (list, tuple))
        if after:
            inner, count = kernel, len(operands)

            def kernel(*refs):
                inner(*refs[:count], *refs[count + len(after) :])

        return pl.pallas_call(
            kernel,
            out_shape=out_shape,
            in_specs=[SMEM] * scalars
            + [HBM] * hbm
            + [VMEM] * (len(operands) - scalars - hbm)
            + [pl.BlockSpec(memory_space=pl.ANY)] * len(after),
            out_specs=[VMEM] * len(out_shape) if several else VMEM,
            scratch_shapes=scratch,
            compiler_params=pltpu.CompilerParams(vmem_limit_bytes=grant),
            cost_estimate=pl.CostEstimate(flops=10**9, bytes_accessed=10**8, transcendentals=0),
        )(*operands, *after)

    def scalar(x):
        return x.reshape(1).astype(jnp.int32)

    odd, even = list(range(1, chips, 2)), list(range(0, chips, 2))
    sent, turned, rest, inputs, rates = call(
        first_kernel,
        [
            shape(len(odd), width + TAIL, rows, dtype=BF16),
            shape(width, tokens, dtype=BF16),
            shape(len(even), tokens, rows, dtype=BF16),
            shape(chips, tokens, rows, dtype=BF16),
            shape(1, width + rows),
        ],
        jnp.stack([core, chip]).astype(jnp.int32),
        *(pltpu.with_memory_space_constraint(x, pltpu.HBM) for x in (out_grads, activations, out_decay, in_decay)),
        scalars=1,
        hbm=4,
        grant=FIRST_GRANT * 2**20,
        scratch=[
            pltpu.VMEM((tokens, width), BF16),
            pltpu.VMEM((len(odd), tokens, rows), BF16),
            pltpu.SemaphoreType.DMA((2 * chips + 3,)),
        ],
    )
    theirs = {1: exchange(sent, "dp", 1)}
    sent = call(rest_kernel, shape(len(even), width + TAIL, rows, dtype=BF16), turned, rest, after=(sent,))
    theirs[0] = exchange(sent, "dp", 1)
    group = [rates, exchange(rates, "layer", 1)]

    levels = [1 << b for b in range(chips.bit_length() - 1)]
    received = [{} for _ in range(split)]
    latest = []

    def blocks(part, offsets, outs, weighs=None, weights=()):
        heard = [[(got, j) for got, j in received[part].get(o, [])] for o in offsets]
        arrays = list({id(got): got for some in heard for got, _ in some}.values())
        picks = [[([id(x) for x in arrays].index(id(got)), j) for got, j in some] for some in heard]
        outs = call(
            functools.partial(sum_kernel, part, offsets, picks, len(arrays), weighs),
            outs,
            turned,
            inputs,
            theirs[offsets[0] % 2],
            *arrays,
            *(weights if weighs else ()),
            after=latest[-1:],
        )
        latest.append(outs[0])
        return outs

    held = []
    for i, level in enumerate(levels):
        offsets = list(range(level, chips, 2 * level))
        soon, held_next = (offsets, []) if level == levels[-1] else (offsets[1:], offsets[:1])
        for part in range(split):
            for at, some in [(level, soon)] + held:
                outs = [shape(len(some), width + TAIL, lanes, dtype=BF16)]
                [sent] = blocks(part, some, outs)
                got = exchange(sent, "dp", 2 * at)
                received[part].update({o ^ at: received[part].get(o ^ at, []) + [(got, j)] for j, o in enumerate(some)})
        held = [(level, held_next)] if held_next else []

    ups, downs = [], []
    below, above = rates, jnp.ones_like(rates)
    for step, size in digits(layers):
        last = step * size == layers
        if step > 1:
            group = [own, exchange(own, "layer", step)]
        if size == 4 and not last:
            group = [jnp.concatenate(group, axis=0)]
            group.append(exchange(group[0], "layer", 2 * step))
        cols, in_rows, *state = call(
            functools.partial(weights_kernel, size, last, len(group)),
            [shape(width, 128), shape(24, rows)] + [shape(3, width + rows)] * (not last),
            scalar(layer // step % size),
            *group,
            below,
            above,
            scalars=1,
            after=latest[-1:],
        )
        if not last:
            own, below, above = state[0][:1], state[0][1:2], state[0][2:]
        for solve, places in zip((ups, downs), weight_places(size, last)):
            solve.append((step, size, cols, in_rows, *places))
    a_own, a_theirs, s_turned = call(
        turn_kernel,
        [shape(chips * rows, rows, dtype=BF16)] * 2 + [shape(width, width, dtype=BF16)],
        scalar(core),
        a_inverse,
        s_inverse,
        scalars=1,
        after=latest[-1:],
    )
    a_theirs = exchange(a_theirs, "dp", 1)

    def steps(solve, value, total, sent, part=0):
        n = value.shape[1]
        for i, (step, size, cols, in_rows, into_value, into_total) in enumerate(solve[:-1]):
            more = i + 1 < len(solve)
            outs = [shape(width, n), message(n)] + [shape(width, n)] * more
            kernel = functools.partial(step_kernel, into_value, into_total, more)
            others = [exchange(sent, "layer", flip * step) for flip in range(1, size)]
            value, sent, total = call(kernel, outs, value, total, cols, in_rows[:, part * n : (part + 1) * n], *others)
        return value, total, sent

    def order_of(solve, part):
        step, size, _, _, orders, place = solve[-1]
        if orders is None:
            return (step,), None, None, place
        (first, second), *places = orders[part % len(orders)]
        return (first * step, second * step), *places

    def cross(solve, part, value, total, sent):
        _, _, cols, in_rows, *_ = solve[-1]
        flips, _, places, _ = order_of(solve, part)
        n = sent.shape[1]
        got = exchange(sent, "layer", flips[0])
        if len(flips) == 1:
            return value, got
        whole = value.shape[1] > n
        at = in_rows if whole or n == rows else in_rows[:, part * n : (part + 1) * n]
        kernel = functools.partial(cross_kernel, places, part if whole else 0)
        value, sent = call(kernel, [shape(width, n), message(n)], value, total, cols, at, got)
        return value, exchange(sent, "layer", flips[1])

    _, _, cols, in_rows, *_ = ups[-1]
    applied = []
    for part in range(split):
        at = in_rows[:, part * lanes : (part + 1) * lanes]
        first = order_of(ups, part)[1] if len(ups) == 1 else None
        sent, value = blocks(part, [0], [message(lanes), shape(width, lanes)], first, (cols, in_rows))
        value, total, sent = steps(ups, value, value, sent, part)
        value, got = cross(ups, part, value, total, sent)
        kernel = functools.partial(side_s_kernel, [order_of(ups, part)[3]])
        applied.append(
            call(kernel, shape(width, lanes, dtype=BF16), value, s_turned, cols, at, got, after=applied[-1:])
        )

    def stack(items, after=()):
        return call(stack_kernel, shape(len(items), width, lanes, dtype=BF16), *items, after=after)

    have = [{0: (rows_of, None)} for rows_of in applied]
    arrivals = [[(part, 0) for part in range(split)]]

    def send(level, batch, after=()):
        items = [have[part][o] for part, o in batch]
        if len(items) == 1 and items[0][1] is None:
            got = exchange(items[0][0], "dp", 2 * level)
        else:
            got = exchange(stack([x if i is None else x[i] for x, i in items], after), "dp", 2 * level)
        came = [(part, o ^ level) for part, o in batch]
        have_of = [(got, i if len(batch) > 1 or items[0][1] is not None else None) for i in range(len(batch))]
        for (part, o), where in zip(came, have_of):
            have[part][o] = where
        return came, got

    for part in range(split):
        for level in reversed(levels[1:]):
            arrivals[0] += send(level, [(part, o) for o in list(have[part])])[0]
    if chips > 1:
        came, got = send(1, [(0, 0)])
        arrivals.append(came)
        for part in range(split):
            batch = [(part, o) for o in list(have[part]) if o > 1 and o % 2 == 0]
            batch += [(part + 1, 0)] if part + 1 < split else []
            if batch:
                came, _ = send(1, batch, [got])
                if part + 1 < split:
                    arrivals[-1] += came
                else:
                    arrivals.append(came)

    own, others, done = None, None, []
    for chosen in arrivals:
        arrays = list({id(have[part][o][0]): have[part][o][0] for part, o in chosen}.values())
        places = jnp.stack([(chip ^ o) * rows + part * lanes for part, o in chosen]).astype(jnp.int32)
        picks = [
            ([id(x) for x in arrays].index(id(have[part][o][0])), have[part][o][1], i)
            for i, (part, o) in enumerate(chosen)
        ]

        def product(a, before, out_shape, after=()):
            before = [] if before is None else [before]
            kernel = functools.partial(side_a_kernel, picks, bool(before))
            return call(kernel, out_shape, places, a, *before, *arrays, scalars=1, after=after)

        final = chosen is arrivals[-1]
        others = product(a_theirs, others, message(rows) if final else shape(width, rows), done)
        own = product(a_own, own, shape(width, rows))
        done = [own]
    others = exchange(others, "dp", 1)

    pieces = split if len(downs) == 1 and downs[-1][1] == 4 else 1
    outs = [shape(width, rows)] * 2 + [message(rows // pieces)] * pieces
    first = [order_of(downs, part)[1] if len(downs) == 1 else None for part in range(pieces)]
    _, _, cols, in_rows, *_ = downs[0]
    value, total, *sent = call(functools.partial(joint_kernel, 0, first), outs, own, others, cols, in_rows)
    if len(downs) > 1:
        value, total, sent[0] = steps(downs, value, total, sent[0])
    operands = [x for part in range(pieces) for x in cross(downs, part, value, total, sent[part])]
    _, _, cols, in_rows, *_ = downs[-1]
    places = [order_of(downs, part)[3] for part in range(pieces)]
    return call(functools.partial(last_kernel, places), shape(1, rows, width, dtype=BF16), cols, in_rows, *operands)


def solution(mesh):
    placed = (
        P("layer", "dp", None),
        P("layer", "dp", None),
        P("layer", "dp", None),
        P("layer", None, None),
        P("layer", "dp"),
        P("layer", None),
    )
    return jax.shard_map(
        shards, mesh=mesh, in_specs=placed, out_specs=P("layer", "dp", None), check_vma=False
    )
```

```python
import functools

import jax
import jax.numpy as jnp
from jax import lax
from jax.experimental import pallas as pl
from jax.experimental.pallas import tpu as pltpu
from jax.sharding import PartitionSpec as P

TAIL = 16
LIFT = 2.0**15
TINY = 1e-30
F32, BF16 = jnp.float32, jnp.bfloat16
VMEM = pl.BlockSpec(memory_space=pltpu.VMEM)
HBM = pl.BlockSpec(memory_space=pltpu.HBM)
FIRST_GRANT = 8
SPLIT = 2


def exchange(x, axis, flip):
    return lax.ppermute(x, axis, [(i, i ^ flip) for i in range(lax.axis_size(axis))])


def put(ref, value):
    rows = value.shape[0]
    top = jnp.maximum(jnp.max(jnp.abs(value), axis=0, keepdims=True), TINY).astype(BF16).astype(F32)
    ref[rows:, :] = jnp.broadcast_to(top, (TAIL, value.shape[1])).astype(BF16)
    z = value * (LIFT / top)
    z2 = z * z
    z4 = z2 * z2
    z8 = z4 * z4
    ref[:rows, :] = jnp.where(z < 0, -z8, z8).astype(BF16)


def get(ref):
    rows = ref.shape[0] - TAIL
    top = ref[rows:, :][:1, :].astype(F32) * (1.0 / LIFT)
    y = ref[:rows, :].astype(F32)
    square = lax.rsqrt(lax.rsqrt(jnp.abs(y) + 1e-37))
    size = square * lax.rsqrt(square)
    return jnp.where(y < 0, -size, size) * top


def core_and_chip():
    place = lax.axis_index("dp")
    return lax.rem(place, 2), lax.div(place, 2)


def first_kernel(
    grads_hbm, inputs_hbm, out_decay, in_decay, sent_ref, turned_ref, rest_ref, own_ref, rates_ref, *scratch
):
    grads_ref, inputs_ref, sems = scratch
    core, chip = core_and_chip()
    width = out_decay.shape[1]
    chips, _, rows = own_ref.shape
    sem = iter(range(sems.shape[0]))

    def copy(source, into):
        out = pltpu.make_async_copy(source, into, sems.at[next(sem)])
        out.start()
        return out

    def load(o, of, into):
        start = pl.multiple_of((2 * (chip ^ o) + of) * rows, rows)
        return copy(inputs_hbm.at[0, :, pl.ds(start, rows)], into)

    lead = copy(grads_hbm.at[0], grads_ref)
    theirs = [load(o, 1 - core, inputs_ref.at[i]) for i, o in enumerate(range(1, chips, 2))]
    others = [load(o, 1 - core, rest_ref.at[i]) for i, o in enumerate(range(0, chips, 2))]
    others += [load(o, core, own_ref.at[o]) for o in range(chips)]
    others.append(copy(out_decay, rates_ref.at[:, pl.ds(0, width)]))
    others.append(copy(in_decay, rates_ref.at[:, pl.ds(width, rows)]))
    lead.wait()
    turned_ref[...] = grads_ref[...].T
    for i, arrival in enumerate(theirs):
        arrival.wait()
        put(sent_ref.at[i], jnp.dot(turned_ref[...], inputs_ref[i], preferred_element_type=F32))
    for arrival in others:
        arrival.wait()


def rest_kernel(turned_ref, inputs_ref, sent_ref, turned_out):
    turned_out[...] = turned_ref[...]
    for i in range(inputs_ref.shape[0]):
        put(sent_ref.at[i], jnp.dot(turned_ref[...], inputs_ref[i], preferred_element_type=F32))


def sum_kernel(part, offsets, picks, n, weighs, passes, turned_ref, own_ref, theirs_ref, *refs):
    messages, outs = refs[:n], refs[n + (2 if weighs else 0) + passes :]
    lanes = outs[0].shape[-1]
    columns = pl.ds(part * lanes, lanes)
    if passes:
        outs[1][...] = refs[n][...]
        outs = outs[:1]
    for i, o in enumerate(offsets):
        total = jnp.dot(turned_ref[...], own_ref[o, :, columns], preferred_element_type=F32)
        total = total + get(theirs_ref.at[o // 2, :, columns])
        for array, j in picks[i]:
            total = total + get(messages[array].at[j])
        if len(outs) > 1:
            outs[1][...] = total
        if weighs:
            cols_ref, rows_ref = refs[n : n + 2]
            total = weight(cols_ref, rows_ref.at[:, columns], weighs) * total
        put(outs[0].at[i] if len(outs[0].shape) == 3 else outs[0], total)


def turn_kernel(a_ref, s_ref, own_ref, send_ref, s_out):
    core, _ = core_and_chip()
    rows = a_ref.shape[1]
    for i in range(own_ref.shape[0] // rows):
        for of, out in ((core, own_ref), (1 - core, send_ref)):
            columns = pl.ds(pl.multiple_of((2 * i + of) * rows, rows), rows)
            out[i * rows : (i + 1) * rows, :] = a_ref[0, :, columns].T
    s_out[...] = s_ref[0].T


def weight(cols_ref, rows_ref, j):
    return cols_ref[:, j : j + 1] * rows_ref[j : j + 1, :]


def weighed(places, cols_ref, rows_ref, messages, value):
    for j, message in zip(places, messages):
        value = value + weight(cols_ref, rows_ref, j) * get(message)
    return value


def step_kernel(into_value, into_total, more, columns, *refs):
    n = len(into_value)
    value_ref, total_ref, cols_ref, rows_ref = refs[:4]
    rows_ref = rows_ref.at[:, columns]
    messages, outs = refs[4 : 4 + n], refs[4 + n :]
    outs[0][...] = weighed(into_value, cols_ref, rows_ref, messages, value_ref[...])
    total = weight(cols_ref, rows_ref, into_total[0]) * total_ref[...]
    total = weighed(into_total[1:], cols_ref, rows_ref, messages, total)
    put(outs[1], total)
    if more:
        outs[2][...] = total


def cross_kernel(places, columns, of, value_ref, total_ref, cols_ref, rows_ref, message_ref, value_out, sent_ref):
    into_value, mix_own, mix_got = places
    at = rows_ref.at[:, columns]
    got = get(message_ref)
    value_out[...] = value_ref[:, of] + weight(cols_ref, at, into_value) * got
    put(sent_ref, weight(cols_ref, at, mix_own) * total_ref[:, of] + weight(cols_ref, at, mix_got) * got)


def side_s_kernel(places, columns, value_ref, s_ref, cols_ref, rows_ref, *refs):
    rows_ref = rows_ref.at[:, columns]
    upper = weighed(places, cols_ref, rows_ref, refs[: len(places)], value_ref[...])
    refs[-1][...] = jnp.dot(s_ref[...], upper.astype(BF16), preferred_element_type=F32).astype(BF16)


def stack_kernel(*refs):
    for i, ref in enumerate(refs[:-1]):
        refs[-1][i] = ref[...]


def side_a_kernel(picks, has_before, *refs):
    refs = list(refs)
    a_ref, (_, chip) = refs.pop(0), core_and_chip()
    solved = refs.pop(0)[...] if has_before else None
    rows = a_ref.shape[1]
    operands, features = [], []
    for array, block, part, o in picks:
        operands.append(refs[array][...] if block is None else refs[array][block])
        lanes = operands[-1].shape[1]
        start = (chip ^ o) * rows + part * lanes
        features.append(a_ref[pl.ds(pl.multiple_of(start, lanes), lanes), :])
    term = jnp.dot(jnp.concatenate(operands, axis=1), jnp.concatenate(features, axis=0), preferred_element_type=F32)
    solved = term if solved is None else solved + term
    if refs[-1].dtype == F32:
        refs[-1][...] = solved
    else:
        put(refs[-1], solved)


def joint_kernel(total_at, sent_at, own_ref, theirs_ref, cols_ref, rows_ref, value_ref, total_ref, *sent_refs):
    value = own_ref[...] + get(theirs_ref)
    value_ref[...] = value
    total_ref[...] = weight(cols_ref, rows_ref, total_at) * value
    for i, sent in enumerate(sent_refs):
        lanes = sent.shape[1]
        columns = slice(i * lanes, (i + 1) * lanes)
        total = total_ref[:, columns]
        if sent_at[i] is not None:
            total = weight(cols_ref, rows_ref.at[:, columns], sent_at[i]) * total
        put(sent, total)


def last_kernel(places, cols_ref, rows_ref, *refs):
    out_ref = refs[-1]
    for i, place in enumerate(places):
        value_ref, message_ref = refs[2 * i : 2 * i + 2]
        lanes = value_ref.shape[1]
        columns = slice(i * lanes, (i + 1) * lanes)
        lower = weighed([place], cols_ref, rows_ref.at[:, columns], [message_ref], value_ref[...])
        out_ref[0, columns, :] = lower.T.astype(BF16)


def digits(layers):
    step, out = 1, []
    while step < layers:
        size = min(4, layers // step)
        out.append((step, size))
        step *= size
    return out


def weights_kernel(step, size, last, n, *refs):
    groups, state = refs[:n], refs[n : n + (2 if step > 1 else 0)]
    cols_ref, rows_ref, *state_ref = refs[n + len(state) :]
    group = [ref[i : i + 1, :] for ref in groups for i in range(ref.shape[0])]
    ones, zeros = jnp.ones_like(group[0]), jnp.zeros_like(group[0])
    below, above = [ref[...] for ref in state] or [group[0], ones]
    mine = lax.rem(lax.div(lax.axis_index("layer"), step), size)

    def product(holds):
        out = ones
        for flip, vector in enumerate(group):
            out = out * jnp.where(holds(me ^ flip), vector, ones)
        return out

    def pick(*cases):
        out = zeros
        for at, vector in cases:
            out = jnp.where(me == at, vector, out)
        return out

    stack = [group[0]]
    for me, factor in ((mine, below), (size - 1 - mine, above)):
        if not last:
            for flip in range(1, size):
                peer = me ^ flip
                between = product(lambda q: (q > me) & (q < peer))
                stack.append(jnp.where(peer > me, factor * between, zeros))
            for flip in range(size):
                stack.append(product(lambda q: q < me ^ flip))
        elif size == 4:
            rates, beside = group[:2]
            far = factor * beside
            stack.append(pick((0, factor), (2, factor)))
            stack.append(pick((2, ones), (3, beside)))
            stack.append(pick((2, rates), (3, ones)))
            stack.append(pick((0, far), (1, factor)))
            stack.append(pick((0, far), (1, factor)))
            stack.append(pick((1, ones), (3, ones)))
            stack.append(pick((0, ones), (1, rates)))
            stack.append(pick((0, factor), (1, factor), (2, factor)))
            stack.append(pick((0, ones), (1, ones), (2, ones), (3, beside)))
        else:
            stack.append(pick((0, factor)))
    width = cols_ref.shape[0]
    stack += [zeros] * (cols_ref.shape[1] - len(stack))
    table = jnp.concatenate(stack, axis=0)
    cols_ref[...] = table[:, :width].T
    rows_ref[...] = table[: rows_ref.shape[0], width:]
    if not last:
        me = mine
        before = product(lambda q: q < me)
        state_ref[0][...] = jnp.concatenate([product(lambda q: q >= 0), below * before, above * before], axis=0)


def weight_places(size, last):
    out = []
    for i in range(2):
        if not last:
            n = 2 * size - 1
            out.append((list(range(1 + i * n, i * n + size)), list(range(i * n + size, 1 + i * n + n))))
        elif size == 4:
            b = 1 + 9 * i
            out.append(([((1, 2), None, (b, b + 1, b + 2), b + 3), ((2, 1), b + 8, (b + 4, b + 5, b + 6), b + 7)], None))
        else:
            out.append((None, 1 + i))
    return out


def shards(activations, out_grads, a_inverse, s_inverse, in_decay, out_decay):
    layers, peers = lax.axis_size("layer"), lax.axis_size("dp")
    chips = peers // 2
    rows = a_inverse.shape[1]
    width = out_grads.shape[2]
    tokens = activations.shape[1]
    split = SPLIT if rows % (128 * SPLIT) == 0 else 1
    lanes = rows // split

    def shape(*dims, dtype=F32):
        return jax.ShapeDtypeStruct(dims, dtype)

    def message(n):
        return shape(width + TAIL, n, dtype=BF16)

    def call(kernel, out_shape, *operands, grant=4 * 2**20, hbm=0, scratch=(), after=()):
        several = isinstance(out_shape, (list, tuple))
        if after:
            inner, count = kernel, len(operands)

            def kernel(*refs):
                inner(*refs[:count], *refs[count + len(after) :])

        return pl.pallas_call(
            kernel,
            out_shape=out_shape,
            in_specs=[HBM] * hbm
            + [VMEM] * (len(operands) - hbm)
            + [pl.BlockSpec(memory_space=pl.ANY)] * len(after),
            out_specs=[VMEM] * len(out_shape) if several else VMEM,
            scratch_shapes=scratch,
            compiler_params=pltpu.CompilerParams(vmem_limit_bytes=grant),
            cost_estimate=pl.CostEstimate(flops=10**9, bytes_accessed=10**8, transcendentals=0),
        )(*operands, *after)

    odd, even = list(range(1, chips, 2)), list(range(0, chips, 2))
    sent, turned, rest, inputs, rates = call(
        first_kernel,
        [
            shape(len(odd), width + TAIL, rows, dtype=BF16),
            shape(width, tokens, dtype=BF16),
            shape(len(even), tokens, rows, dtype=BF16),
            shape(chips, tokens, rows, dtype=BF16),
            shape(1, width + rows),
        ],
        *(pltpu.with_memory_space_constraint(x, pltpu.HBM) for x in (out_grads, activations, out_decay, in_decay)),
        hbm=4,
        grant=FIRST_GRANT * 2**20,
        scratch=[
            pltpu.VMEM((tokens, width), BF16),
            pltpu.VMEM((len(odd), tokens, rows), BF16),
            pltpu.SemaphoreType.DMA((2 * chips + 3,)),
        ],
    )
    theirs = {1: exchange(sent, "dp", 1)}
    outs = [shape(len(even), width + TAIL, rows, dtype=BF16), shape(width, tokens, dtype=BF16)]
    sent, turned = call(rest_kernel, outs, turned, rest, after=(sent,))
    theirs[0] = exchange(sent, "dp", 1)

    levels = [1 << b for b in range(chips.bit_length() - 1)]
    received = [{} for _ in range(split)]
    latest = []

    def blocks(part, offsets, outs, weighs=None, weights=(), passed=()):
        heard = [[(got, j) for got, j in received[part].get(o, [])] for o in offsets]
        arrays = list({id(got): got for some in heard for got, _ in some}.values())
        picks = [[([id(x) for x in arrays].index(id(got)), j) for got, j in some] for some in heard]
        outs = call(
            functools.partial(sum_kernel, part, offsets, picks, len(arrays), weighs, len(passed)),
            outs,
            turned,
            inputs,
            theirs[offsets[0] % 2],
            *arrays,
            *(weights if weighs else ()),
            *passed,
            after=latest[-1:],
        )
        latest.append(outs[0])
        return outs

    held = []
    for i, level in enumerate(levels):
        offsets = list(range(level, chips, 2 * level))
        soon, held_next = (offsets, []) if level == levels[-1] else (offsets[1:], offsets[:1])
        for part in range(split):
            for at, some in [(level, soon)] + held:
                outs = [shape(len(some), width + TAIL, lanes, dtype=BF16)]
                final = len(latest) + 1 == split * (2 * len(levels) - 1)
                sent, *passed = blocks(part, some, outs + [shape(1, width + rows)] * final, passed=[rates] * final)
                rates = passed[0] if final else rates
                got = exchange(sent, "dp", 2 * at)
                received[part].update({o ^ at: received[part].get(o ^ at, []) + [(got, j)] for j, o in enumerate(some)})
        held = [(level, held_next)] if held_next else []

    group = [rates, exchange(rates, "layer", 1)]
    ups, downs = [], []
    state = []
    for step, size in digits(layers):
        last = step * size == layers
        if step > 1:
            group = [own, exchange(own, "layer", step)]
        if size == 4 and not last:
            group = [jnp.concatenate(group, axis=0)]
            group.append(exchange(group[0], "layer", 2 * step))
        cols, in_rows, *new = call(
            functools.partial(weights_kernel, step, size, last, len(group)),
            [shape(width, 128), shape(24, rows)] + [shape(3, width + rows)] * (not last),
            *group,
            *state,
            after=latest[-1:],
        )
        if not last:
            own, state = new[0][:1], [new[0][1:2], new[0][2:]]
        for solve, places in zip((ups, downs), weight_places(size, last)):
            solve.append((step, size, cols, in_rows, *places))
    a_own, a_theirs, s_turned = call(
        turn_kernel,
        [shape(chips * rows, rows, dtype=BF16)] * 2 + [shape(width, width, dtype=BF16)],
        a_inverse,
        s_inverse,
        after=latest[-1:],
    )
    a_theirs = exchange(a_theirs, "dp", 1)

    def steps(solve, value, total, sent, part=0):
        n = value.shape[1]
        for i, (step, size, cols, in_rows, into_value, into_total) in enumerate(solve[:-1]):
            more = i + 1 < len(solve)
            outs = [shape(width, n), message(n)] + [shape(width, n)] * more
            kernel = functools.partial(step_kernel, into_value, into_total, more, pl.ds(part * n, n))
            others = [exchange(sent, "layer", flip * step) for flip in range(1, size)]
            value, sent, *total = call(kernel, outs, value, total, cols, in_rows, *others)
            total = total[0] if more else value
        return value, total, sent

    def order_of(solve, part):
        step, size, _, _, orders, place = solve[-1]
        if orders is None:
            return (step,), None, None, place
        (first, second), *places = orders[part % len(orders)]
        return (first * step, second * step), *places

    def cross(solve, part, value, total, sent):
        _, _, cols, in_rows, *_ = solve[-1]
        flips, _, places, _ = order_of(solve, part)
        n = sent.shape[1]
        got = exchange(sent, "layer", flips[0])
        if len(flips) == 1:
            return value, got
        columns = slice(part * n, (part + 1) * n)
        of = columns if value.shape[1] > n else slice(0, n)
        kernel = functools.partial(cross_kernel, places, columns, of)
        value, sent = call(kernel, [shape(width, n), message(n)], value, total, cols, in_rows, got)
        return value, exchange(sent, "layer", flips[1])

    _, _, cols, in_rows, *_ = ups[-1]
    applied = []
    for part in range(split):
        first = order_of(ups, part)[1] if len(ups) == 1 else None
        sent, value = blocks(part, [0], [message(lanes), shape(width, lanes)], first, (cols, in_rows))
        value, total, sent = steps(ups, value, value, sent, part)
        value, got = cross(ups, part, value, total, sent)
        kernel = functools.partial(side_s_kernel, [order_of(ups, part)[3]], slice(part * lanes, (part + 1) * lanes))
        applied.append(
            call(kernel, shape(width, lanes, dtype=BF16), value, s_turned, cols, in_rows, got, after=applied[-1:])
        )

    def stack(items, after=()):
        return call(stack_kernel, shape(len(items), width, lanes, dtype=BF16), *items, after=after)

    have = [{0: (rows_of, None)} for rows_of in applied]
    arrivals = [[(part, 0) for part in range(split)]]

    def send(level, batch, after=()):
        items = [have[part][o] for part, o in batch]
        if len(items) == 1 and not after:
            got = exchange(items[0][0], "dp", 2 * level)
        else:
            got = exchange(stack([x if i is None else x[i] for x, i in items], after), "dp", 2 * level)
        came = [(part, o ^ level) for part, o in batch]
        have_of = [(got, i if len(batch) > 1 or after else None) for i in range(len(batch))]
        for (part, o), where in zip(came, have_of):
            have[part][o] = where
        return came, got

    for part in range(split):
        for level in reversed(levels[1:]):
            arrivals[0] += send(level, [(part, o) for o in list(have[part])])[0]
    if chips > 1:
        plan = [[(part, 0)] for part in range(split)]
        plan += [[(part, o) for o in have[part] if o > 1] for part in range(split)]
        plan = [batch for batch in plan if batch]
        gots = []
        for i, batch in enumerate(plan):
            came, got = send(1, batch, gots[:1] if i == split else [])
            gots.append(got)
            if i + 1 < len(plan) and i:
                arrivals[-1] += came
            else:
                arrivals.append(came)

    own, others, done = None, None, []
    for chosen in arrivals:
        arrays = list({id(have[part][o][0]): have[part][o][0] for part, o in chosen}.values())
        picks = [([id(x) for x in arrays].index(id(have[part][o][0])), have[part][o][1], part, o) for part, o in chosen]

        def product(a, before, out_shape, after=()):
            before = [] if before is None else [before]
            kernel = functools.partial(side_a_kernel, picks, bool(before))
            return call(kernel, out_shape, a, *before, *arrays, after=after)

        final = chosen is arrivals[-1]
        others = product(a_theirs, others, message(rows) if final else shape(width, rows), done)
        own = product(a_own, own, shape(width, rows))
        done = [own]
    others = exchange(others, "dp", 1)

    pieces = split if len(downs) == 1 and downs[-1][1] == 4 else 1
    outs = [shape(width, rows)] * 2 + [message(rows // pieces)] * pieces
    first = [order_of(downs, part)[1] if len(downs) == 1 else None for part in range(pieces)]
    _, _, cols, in_rows, *_ = downs[0]
    value, total, *sent = call(functools.partial(joint_kernel, 0, first), outs, own, others, cols, in_rows)
    if len(downs) > 1:
        value, total, sent[0] = steps(downs, value, total, sent[0])
    operands = [x for part in range(pieces) for x in cross(downs, part, value, total, sent[part])]
    _, _, cols, in_rows, *_ = downs[-1]
    places = [order_of(downs, part)[3] for part in range(pieces)]
    return call(functools.partial(last_kernel, places), shape(1, rows, width, dtype=BF16), cols, in_rows, *operands)


def solution(mesh):
    placed = (
        P("layer", "dp", None),
        P("layer", "dp", None),
        P("layer", "dp", None),
        P("layer", None, None),
        P("layer", "dp"),
        P("layer", None),
    )
    return jax.shard_map(
        shards, mesh=mesh, in_specs=placed, out_specs=P("layer", "dp", None), check_vma=False
    )
```

```python
import functools

import jax
import jax.numpy as jnp
from jax import lax
from jax.experimental import pallas as pl
from jax.experimental.pallas import tpu as pltpu
from jax.sharding import PartitionSpec as P

TAIL = 16
LIFT = 2.0**15
TINY = 1e-30
F32, BF16 = jnp.float32, jnp.bfloat16
VMEM = pl.BlockSpec(memory_space=pltpu.VMEM)
HBM = pl.BlockSpec(memory_space=pltpu.HBM)
FIRST_GRANT = 8
SPLIT = 2


def exchange(x, axis, flip):
    return lax.ppermute(x, axis, [(i, i ^ flip) for i in range(lax.axis_size(axis))])


def put(ref, value):
    rows = value.shape[0]
    top = jnp.maximum(jnp.max(jnp.abs(value), axis=0, keepdims=True), TINY).astype(BF16).astype(F32)
    ref[rows:, :] = jnp.broadcast_to(top, (TAIL, value.shape[1])).astype(BF16)
    z = value * (LIFT / top)
    z2 = z * z
    z4 = z2 * z2
    z8 = z4 * z4
    ref[:rows, :] = jnp.where(z < 0, -z8, z8).astype(BF16)


def get(ref):
    rows = ref.shape[0] - TAIL
    top = ref[rows:, :][:1, :].astype(F32) * (1.0 / LIFT)
    y = ref[:rows, :].astype(F32)
    square = lax.rsqrt(lax.rsqrt(jnp.abs(y) + 1e-37))
    size = square * lax.rsqrt(square)
    return jnp.where(y < 0, -top, top) * size


def core_and_chip():
    place = lax.axis_index("dp")
    return lax.rem(place, 2), lax.div(place, 2)


def first_kernel(
    grads_hbm, inputs_hbm, out_decay, in_decay, sent_ref, turned_ref, rest_ref, own_ref, rates_ref, *scratch
):
    grads_ref, inputs_ref, sems = scratch
    core, chip = core_and_chip()
    width = out_decay.shape[1]
    chips, _, rows = own_ref.shape
    sem = iter(range(sems.shape[0]))

    def copy(source, into):
        out = pltpu.make_async_copy(source, into, sems.at[next(sem)])
        out.start()
        return out

    def load(o, of, into):
        start = pl.multiple_of((2 * (chip ^ o) + of) * rows, rows)
        return copy(inputs_hbm.at[0, :, pl.ds(start, rows)], into)

    lead = copy(grads_hbm.at[0], grads_ref)
    theirs = [load(o, 1 - core, inputs_ref.at[i]) for i, o in enumerate(range(1, chips, 2))]
    others = [load(o, 1 - core, rest_ref.at[i]) for i, o in enumerate(range(0, chips, 2))]
    others += [load(o, core, own_ref.at[o]) for o in range(chips)]
    others.append(copy(out_decay, rates_ref.at[:, pl.ds(0, width)]))
    others.append(copy(in_decay, rates_ref.at[:, pl.ds(width, rows)]))
    lead.wait()
    turned_ref[...] = grads_ref[...].T
    for i, arrival in enumerate(theirs):
        arrival.wait()
        put(sent_ref.at[i], jnp.dot(turned_ref[...], inputs_ref[i], preferred_element_type=F32))
    for arrival in others:
        arrival.wait()


def rest_kernel(turned_ref, inputs_ref, sent_ref, turned_out):
    turned_out[...] = turned_ref[...]
    for i in range(inputs_ref.shape[0]):
        put(sent_ref.at[i], jnp.dot(turned_ref[...], inputs_ref[i], preferred_element_type=F32))


def sum_kernel(part, offsets, picks, n, weighs, passes, turned_ref, own_ref, theirs_ref, *refs):
    messages, outs = refs[:n], refs[n + (2 if weighs else 0) + passes :]
    lanes = outs[0].shape[-1]
    columns = pl.ds(part * lanes, lanes)
    if passes:
        outs[1][...] = refs[n][...]
        outs = outs[:1]
    for i, o in enumerate(offsets):
        total = jnp.dot(turned_ref[...], own_ref[o, :, columns], preferred_element_type=F32)
        total = total + get(theirs_ref.at[o // 2, :, columns])
        for array, j in picks[i]:
            total = total + get(messages[array].at[j])
        if len(outs) > 1:
            outs[1][...] = total
        if weighs:
            cols_ref, rows_ref = refs[n : n + 2]
            total = weight(cols_ref, rows_ref.at[:, columns], weighs) * total
        put(outs[0].at[i] if len(outs[0].shape) == 3 else outs[0], total)


def turn_kernel(a_ref, s_ref, own_ref, send_ref, s_out):
    core, _ = core_and_chip()
    rows = a_ref.shape[1]
    for i in range(own_ref.shape[0] // rows):
        for of, out in ((core, own_ref), (1 - core, send_ref)):
            columns = pl.ds(pl.multiple_of((2 * i + of) * rows, rows), rows)
            out[i * rows : (i + 1) * rows, :] = a_ref[0, :, columns].T
    s_out[...] = s_ref[0].T


def weight(cols_ref, rows_ref, j):
    return cols_ref[:, j : j + 1] * rows_ref[j : j + 1, :]


def weighed(places, cols_ref, rows_ref, messages, value):
    for j, message in zip(places, messages):
        value = value + weight(cols_ref, rows_ref, j) * get(message)
    return value


def step_kernel(into_value, into_total, more, columns, *refs):
    n = len(into_value)
    value_ref, total_ref, cols_ref, rows_ref = refs[:4]
    rows_ref = rows_ref.at[:, columns]
    messages, outs = refs[4 : 4 + n], refs[4 + n :]
    outs[0][...] = weighed(into_value, cols_ref, rows_ref, messages, value_ref[...])
    total = weight(cols_ref, rows_ref, into_total[0]) * total_ref[...]
    total = weighed(into_total[1:], cols_ref, rows_ref, messages, total)
    put(outs[1], total)
    if more:
        outs[2][...] = total


def cross_kernel(places, columns, of, value_ref, total_ref, cols_ref, rows_ref, message_ref, value_out, sent_ref):
    into_value, mix_own, mix_got = places
    at = rows_ref.at[:, columns]
    got = get(message_ref)
    value_out[...] = value_ref[:, of] + weight(cols_ref, at, into_value) * got
    put(sent_ref, weight(cols_ref, at, mix_own) * total_ref[:, of] + weight(cols_ref, at, mix_got) * got)


def side_s_kernel(places, columns, value_ref, s_ref, cols_ref, rows_ref, *refs):
    rows_ref = rows_ref.at[:, columns]
    upper = weighed(places, cols_ref, rows_ref, refs[: len(places)], value_ref[...])
    refs[-1][...] = jnp.dot(s_ref[...], upper.astype(BF16), preferred_element_type=F32).astype(BF16)


def stack_kernel(*refs):
    for i, ref in enumerate(refs[:-1]):
        refs[-1][i] = ref[...]


def side_a_kernel(picks, has_before, *refs):
    refs = list(refs)
    a_ref, (_, chip) = refs.pop(0), core_and_chip()
    solved = refs.pop(0)[...] if has_before else None
    rows = a_ref.shape[1]
    operands, features = [], []
    for array, block, part, o in picks:
        operands.append(refs[array][...] if block is None else refs[array][block])
        lanes = operands[-1].shape[1]
        start = (chip ^ o) * rows + part * lanes
        features.append(a_ref[pl.ds(pl.multiple_of(start, lanes), lanes), :])
    term = jnp.dot(jnp.concatenate(operands, axis=1), jnp.concatenate(features, axis=0), preferred_element_type=F32)
    solved = term if solved is None else solved + term
    if refs[-1].dtype == F32:
        refs[-1][...] = solved
    else:
        put(refs[-1], solved)


def joint_kernel(total_at, sent_at, own_ref, theirs_ref, cols_ref, rows_ref, value_ref, total_ref, *sent_refs):
    value = own_ref[...] + get(theirs_ref)
    value_ref[...] = value
    total_ref[...] = weight(cols_ref, rows_ref, total_at) * value
    for i, sent in enumerate(sent_refs):
        lanes = sent.shape[1]
        columns = slice(i * lanes, (i + 1) * lanes)
        total = total_ref[:, columns]
        if sent_at[i] is not None:
            total = weight(cols_ref, rows_ref.at[:, columns], sent_at[i]) * total
        put(sent, total)


def last_kernel(places, cols_ref, rows_ref, *refs):
    out_ref, turned_ref, sems = refs[-3:]
    copies = []
    for i, place in enumerate(places):
        value_ref, message_ref = refs[2 * i : 2 * i + 2]
        lanes = value_ref.shape[1]
        columns = slice(i * lanes, (i + 1) * lanes)
        lower = weighed([place], cols_ref, rows_ref.at[:, columns], [message_ref], value_ref[...])
        turned_ref[columns, :] = lower.astype(BF16).T
        rows = pl.ds(i * lanes, lanes)
        copies.append(pltpu.make_async_copy(turned_ref.at[rows], out_ref.at[0, rows], sems.at[i]))
        copies[-1].start()
    for copy in copies:
        copy.wait()


def digits(layers):
    step, out = 1, []
    while step < layers:
        size = min(4, layers // step)
        out.append((step, size))
        step *= size
    return out


def weights_kernel(step, size, last, n, *refs):
    groups, state = refs[:n], refs[n : n + (2 if step > 1 else 0)]
    cols_ref, rows_ref, *state_ref = refs[n + len(state) :]
    group = [ref[i : i + 1, :] for ref in groups for i in range(ref.shape[0])]
    ones, zeros = jnp.ones_like(group[0]), jnp.zeros_like(group[0])
    below, above = [ref[...] for ref in state] or [group[0], ones]
    mine = lax.rem(lax.div(lax.axis_index("layer"), step), size)

    def product(holds):
        out = ones
        for flip, vector in enumerate(group):
            out = out * jnp.where(holds(me ^ flip), vector, ones)
        return out

    def pick(*cases):
        out = zeros
        for at, vector in cases:
            out = jnp.where(me == at, vector, out)
        return out

    stack = [group[0]]
    for me, factor in ((mine, below), (size - 1 - mine, above)):
        if not last:
            for flip in range(1, size):
                peer = me ^ flip
                between = product(lambda q: (q > me) & (q < peer))
                stack.append(jnp.where(peer > me, factor * between, zeros))
            for flip in range(size):
                stack.append(product(lambda q: q < me ^ flip))
        elif size == 4:
            rates, beside = group[:2]
            far = factor * beside
            stack.append(pick((0, factor), (2, factor)))
            stack.append(pick((2, ones), (3, beside)))
            stack.append(pick((2, rates), (3, ones)))
            stack.append(pick((0, far), (1, factor)))
            stack.append(pick((0, far), (1, factor)))
            stack.append(pick((1, ones), (3, ones)))
            stack.append(pick((0, ones), (1, rates)))
            stack.append(pick((0, factor), (1, factor), (2, factor)))
            stack.append(pick((0, ones), (1, ones), (2, ones), (3, beside)))
        else:
            stack.append(pick((0, factor)))
    width = cols_ref.shape[0]
    stack += [zeros] * (cols_ref.shape[1] - len(stack))
    table = jnp.concatenate(stack, axis=0)
    cols_ref[...] = table[:, :width].T
    rows_ref[...] = table[: rows_ref.shape[0], width:]
    if not last:
        me = mine
        before = product(lambda q: q < me)
        state_ref[0][...] = jnp.concatenate([product(lambda q: q >= 0), below * before, above * before], axis=0)


def weight_places(size, last):
    out = []
    for i in range(2):
        if not last:
            n = 2 * size - 1
            out.append((list(range(1 + i * n, i * n + size)), list(range(i * n + size, 1 + i * n + n))))
        elif size == 4:
            b = 1 + 9 * i
            out.append(([((1, 2), None, (b, b + 1, b + 2), b + 3), ((2, 1), b + 8, (b + 4, b + 5, b + 6), b + 7)], None))
        else:
            out.append((None, 1 + i))
    return out


def shards(activations, out_grads, a_inverse, s_inverse, in_decay, out_decay):
    layers, peers = lax.axis_size("layer"), lax.axis_size("dp")
    chips = peers // 2
    rows = a_inverse.shape[1]
    width = out_grads.shape[2]
    tokens = activations.shape[1]
    split = SPLIT if rows % (128 * SPLIT) == 0 else 1
    lanes = rows // split

    def shape(*dims, dtype=F32):
        return jax.ShapeDtypeStruct(dims, dtype)

    def message(n):
        return shape(width + TAIL, n, dtype=BF16)

    def call(kernel, out_shape, *operands, grant=4 * 2**20, hbm=0, scratch=(), after=(), anywhere=False):
        several = isinstance(out_shape, (list, tuple))
        if after:
            inner, count = kernel, len(operands)

            def kernel(*refs):
                inner(*refs[:count], *refs[count + len(after) :])

        return pl.pallas_call(
            kernel,
            out_shape=out_shape,
            in_specs=[HBM] * hbm
            + [VMEM] * (len(operands) - hbm)
            + [pl.BlockSpec(memory_space=pl.ANY)] * len(after),
            out_specs=[VMEM] * len(out_shape) if several else pl.BlockSpec(memory_space=pl.ANY) if anywhere else VMEM,
            scratch_shapes=scratch,
            compiler_params=pltpu.CompilerParams(vmem_limit_bytes=grant),
            cost_estimate=pl.CostEstimate(flops=12 * 10**8, bytes_accessed=10**8, transcendentals=0),
        )(*operands, *after)

    odd, even = list(range(1, chips, 2)), list(range(0, chips, 2))
    sent, turned, rest, inputs, rates = call(
        first_kernel,
        [
            shape(len(odd), width + TAIL, rows, dtype=BF16),
            shape(width, tokens, dtype=BF16),
            shape(len(even), tokens, rows, dtype=BF16),
            shape(chips, tokens, rows, dtype=BF16),
            shape(1, width + rows),
        ],
        *(pltpu.with_memory_space_constraint(x, pltpu.HBM) for x in (out_grads, activations, out_decay, in_decay)),
        hbm=4,
        grant=FIRST_GRANT * 2**20,
        scratch=[
            pltpu.VMEM((tokens, width), BF16),
            pltpu.VMEM((len(odd), tokens, rows), BF16),
            pltpu.SemaphoreType.DMA((2 * chips + 3,)),
        ],
    )
    theirs = {1: exchange(sent, "dp", 1)}
    outs = [shape(len(even), width + TAIL, rows, dtype=BF16), shape(width, tokens, dtype=BF16)]
    sent, turned = call(rest_kernel, outs, turned, rest, after=(sent,))
    theirs[0] = exchange(sent, "dp", 1)

    levels = [1 << b for b in range(chips.bit_length() - 1)]
    received = [{} for _ in range(split)]
    latest = []

    def blocks(part, offsets, outs, weighs=None, weights=(), passed=()):
        heard = [[(got, j) for got, j in received[part].get(o, [])] for o in offsets]
        arrays = list({id(got): got for some in heard for got, _ in some}.values())
        picks = [[([id(x) for x in arrays].index(id(got)), j) for got, j in some] for some in heard]
        outs = call(
            functools.partial(sum_kernel, part, offsets, picks, len(arrays), weighs, len(passed)),
            outs,
            turned,
            inputs,
            theirs[offsets[0] % 2],
            *arrays,
            *(weights if weighs else ()),
            *passed,
            after=latest[-1:],
        )
        latest.append(outs[0])
        return outs

    held = []
    for i, level in enumerate(levels):
        offsets = list(range(level, chips, 2 * level))
        soon, held_next = (offsets, []) if level == levels[-1] else (offsets[1:], offsets[:1])
        for part in range(split):
            for at, some in [(level, soon)] + held:
                outs = [shape(len(some), width + TAIL, lanes, dtype=BF16)]
                final = len(latest) + 1 == split * (2 * len(levels) - 1)
                sent, *passed = blocks(part, some, outs + [shape(1, width + rows)] * final, passed=[rates] * final)
                rates = passed[0] if final else rates
                got = exchange(sent, "dp", 2 * at)
                received[part].update({o ^ at: received[part].get(o ^ at, []) + [(got, j)] for j, o in enumerate(some)})
        held = [(level, held_next)] if held_next else []

    group = [rates, exchange(rates, "layer", 1)]
    ups, downs = [], []
    state = []
    for step, size in digits(layers):
        last = step * size == layers
        if step > 1:
            group = [own, exchange(own, "layer", step)]
        if size == 4 and not last:
            group = [jnp.concatenate(group, axis=0)]
            group.append(exchange(group[0], "layer", 2 * step))
        cols, in_rows, *new = call(
            functools.partial(weights_kernel, step, size, last, len(group)),
            [shape(width, 128), shape(24, rows)] + [shape(3, width + rows)] * (not last),
            *group,
            *state,
            after=latest[-1:],
        )
        if not last:
            own, state = new[0][:1], [new[0][1:2], new[0][2:]]
        for solve, places in zip((ups, downs), weight_places(size, last)):
            solve.append((step, size, cols, in_rows, *places))
    a_own, a_theirs, s_turned = call(
        turn_kernel,
        [shape(chips * rows, rows, dtype=BF16)] * 2 + [shape(width, width, dtype=BF16)],
        a_inverse,
        s_inverse,
        after=latest[-1:],
    )
    a_theirs = exchange(a_theirs, "dp", 1)

    def steps(solve, value, total, sent, part=0):
        n = value.shape[1]
        for i, (step, size, cols, in_rows, into_value, into_total) in enumerate(solve[:-1]):
            more = i + 1 < len(solve)
            outs = [shape(width, n), message(n)] + [shape(width, n)] * more
            kernel = functools.partial(step_kernel, into_value, into_total, more, pl.ds(part * n, n))
            others = [exchange(sent, "layer", flip * step) for flip in range(1, size)]
            value, sent, *total = call(kernel, outs, value, total, cols, in_rows, *others)
            total = total[0] if more else value
        return value, total, sent

    def order_of(solve, part):
        step, size, _, _, orders, place = solve[-1]
        if orders is None:
            return (step,), None, None, place
        (first, second), *places = orders[part % len(orders)]
        return (first * step, second * step), *places

    def cross(solve, part, value, total, sent):
        _, _, cols, in_rows, *_ = solve[-1]
        flips, _, places, _ = order_of(solve, part)
        n = sent.shape[1]
        got = exchange(sent, "layer", flips[0])
        if len(flips) == 1:
            return value, got
        columns = slice(part * n, (part + 1) * n)
        of = columns if value.shape[1] > n else slice(0, n)
        kernel = functools.partial(cross_kernel, places, columns, of)
        value, sent = call(kernel, [shape(width, n), message(n)], value, total, cols, in_rows, got)
        return value, exchange(sent, "layer", flips[1])

    _, _, cols, in_rows, *_ = ups[-1]
    applied = []
    for part in range(split):
        first = order_of(ups, part)[1] if len(ups) == 1 else None
        sent, value = blocks(part, [0], [message(lanes), shape(width, lanes)], first, (cols, in_rows))
        value, total, sent = steps(ups, value, value, sent, part)
        value, got = cross(ups, part, value, total, sent)
        kernel = functools.partial(side_s_kernel, [order_of(ups, part)[3]], slice(part * lanes, (part + 1) * lanes))
        applied.append(
            call(kernel, shape(width, lanes, dtype=BF16), value, s_turned, cols, in_rows, got, after=applied[-1:])
        )

    def stack(items, after=()):
        return call(stack_kernel, shape(len(items), width, lanes, dtype=BF16), *items, after=after)

    have = [{0: (rows_of, None)} for rows_of in applied]
    arrivals = [[(part, 0) for part in range(split)]]

    def send(level, batch, after=()):
        items = [have[part][o] for part, o in batch]
        if len(items) == 1 and not after:
            got = exchange(items[0][0], "dp", 2 * level)
        else:
            got = exchange(stack([x if i is None else x[i] for x, i in items], after), "dp", 2 * level)
        came = [(part, o ^ level) for part, o in batch]
        have_of = [(got, i if len(batch) > 1 or after else None) for i in range(len(batch))]
        for (part, o), where in zip(came, have_of):
            have[part][o] = where
        return came, got

    for part in range(split):
        for level in reversed(levels[1:]):
            arrivals[0] += send(level, [(part, o) for o in list(have[part])])[0]
    if chips > 1:
        plan = [[(part, 0)] for part in range(split)]
        plan += [[(part, o) for o in have[part] if o > 1] for part in range(split)]
        plan = [batch for batch in plan if batch]
        gots = []
        for i, batch in enumerate(plan):
            came, got = send(1, batch, gots[:1] if i == split else [])
            gots.append(got)
            if i + 1 < len(plan) and i:
                arrivals[-1] += came
            else:
                arrivals.append(came)

    own, others, done = None, None, []
    for chosen in arrivals:
        arrays = list({id(have[part][o][0]): have[part][o][0] for part, o in chosen}.values())
        picks = [([id(x) for x in arrays].index(id(have[part][o][0])), have[part][o][1], part, o) for part, o in chosen]

        def product(a, before, out_shape, after=()):
            before = [] if before is None else [before]
            kernel = functools.partial(side_a_kernel, picks, bool(before))
            return call(kernel, out_shape, a, *before, *arrays, after=after)

        final = chosen is arrivals[-1]
        others = product(a_theirs, others, message(rows) if final else shape(width, rows), done)
        own = product(a_own, own, shape(width, rows))
        done = [own]
    others = exchange(others, "dp", 1)

    pieces = split if len(downs) == 1 and downs[-1][1] == 4 else 1
    outs = [shape(width, rows)] * 2 + [message(rows // pieces)] * pieces
    first = [order_of(downs, part)[1] if len(downs) == 1 else None for part in range(pieces)]
    _, _, cols, in_rows, *_ = downs[0]
    value, total, *sent = call(functools.partial(joint_kernel, 0, first), outs, own, others, cols, in_rows)
    if len(downs) > 1:
        value, total, sent[0] = steps(downs, value, total, sent[0])
    operands = [x for part in range(pieces) for x in cross(downs, part, value, total, sent[part])]
    _, _, cols, in_rows, *_ = downs[-1]
    places = [order_of(downs, part)[3] for part in range(pieces)]
    return call(
        functools.partial(last_kernel, places),
        shape(1, rows, width, dtype=BF16),
        cols,
        in_rows,
        *operands,
        scratch=[pltpu.VMEM((rows, width), BF16), pltpu.SemaphoreType.DMA((len(places),))],
        anywhere=True,
    )


def solution(mesh):
    placed = (
        P("layer", "dp", None),
        P("layer", "dp", None),
        P("layer", "dp", None),
        P("layer", None, None),
        P("layer", "dp"),
        P("layer", None),
    )
    return jax.shard_map(
        shards, mesh=mesh, in_specs=placed, out_specs=P("layer", "dp", None), check_vma=False
    )
```

```python
import functools

import jax
import jax.numpy as jnp
from jax import lax
from jax.experimental import pallas as pl
from jax.experimental.pallas import tpu as pltpu
from jax.sharding import PartitionSpec as P

TAIL = 16
LIFT = 2.0**15
TINY = 1e-30
F32, BF16 = jnp.float32, jnp.bfloat16
VMEM = pl.BlockSpec(memory_space=pltpu.VMEM)
HBM = pl.BlockSpec(memory_space=pltpu.HBM)
FIRST_GRANT = 8
SPLIT = 2


def exchange(x, axis, flip):
    return lax.ppermute(x, axis, [(i, i ^ flip) for i in range(lax.axis_size(axis))])


def put(ref, value):
    rows = value.shape[0]
    top = jnp.maximum(jnp.max(jnp.abs(value), axis=0, keepdims=True), TINY).astype(BF16).astype(F32)
    ref[rows:, :] = jnp.broadcast_to(top, (TAIL, value.shape[1])).astype(BF16)
    z = value * (LIFT / top)
    z2 = z * z
    z4 = z2 * z2
    z8 = z4 * z4
    ref[:rows, :] = jnp.where(z < 0, -z8, z8).astype(BF16)


def get(ref):
    rows = ref.shape[0] - TAIL
    top = ref[rows:, :][:1, :].astype(F32) * (1.0 / LIFT)
    y = ref[:rows, :].astype(F32)
    square = lax.rsqrt(lax.rsqrt(jnp.abs(y) + 1e-37))
    size = square * lax.rsqrt(square)
    return jnp.where(y < 0, -top, top) * size


def core_and_chip():
    place = lax.axis_index("dp")
    return lax.rem(place, 2), lax.div(place, 2)


def first_kernel(
    grads_hbm, inputs_hbm, out_decay, in_decay, sent_ref, turned_ref, rest_ref, own_ref, rates_ref, *scratch
):
    grads_ref, inputs_ref, sems = scratch
    core, chip = core_and_chip()
    width = out_decay.shape[1]
    chips, _, rows = own_ref.shape
    sem = iter(range(sems.shape[0]))

    def copy(source, into):
        out = pltpu.make_async_copy(source, into, sems.at[next(sem)])
        out.start()
        return out

    def load(o, of, into):
        start = pl.multiple_of((2 * (chip ^ o) + of) * rows, rows)
        return copy(inputs_hbm.at[0, :, pl.ds(start, rows)], into)

    lead = copy(grads_hbm.at[0], grads_ref)
    theirs = [load(o, 1 - core, inputs_ref.at[i]) for i, o in enumerate(range(1, chips, 2))]
    others = [load(o, 1 - core, rest_ref.at[i]) for i, o in enumerate(range(0, chips, 2))]
    others += [load(o, core, own_ref.at[o]) for o in range(chips)]
    others.append(copy(out_decay, rates_ref.at[:, pl.ds(0, width)]))
    others.append(copy(in_decay, rates_ref.at[:, pl.ds(width, rows)]))
    lead.wait()
    turned_ref[...] = grads_ref[...].T
    for i, arrival in enumerate(theirs):
        arrival.wait()
        put(sent_ref.at[i], jnp.dot(turned_ref[...], inputs_ref[i], preferred_element_type=F32))
    for arrival in others:
        arrival.wait()


def rest_kernel(turned_ref, inputs_ref, sent_ref, turned_out):
    turned_out[...] = turned_ref[...]
    for i in range(inputs_ref.shape[0]):
        put(sent_ref.at[i], jnp.dot(turned_ref[...], inputs_ref[i], preferred_element_type=F32))


def sum_kernel(part, offsets, picks, n, weighs, passes, turned_ref, own_ref, theirs_ref, *refs):
    messages, outs = refs[:n], refs[n + (2 if weighs else 0) + passes :]
    lanes = outs[0].shape[-1]
    columns = pl.ds(part * lanes, lanes)
    if passes:
        outs[1][...] = refs[n][...]
        outs = outs[:1]
    for i, o in enumerate(offsets):
        total = jnp.dot(turned_ref[...], own_ref[o, :, columns], preferred_element_type=F32)
        total = total + get(theirs_ref.at[o // 2, :, columns])
        for array, j in picks[i]:
            total = total + get(messages[array].at[j])
        if len(outs) > 1:
            outs[1][...] = total
        if weighs:
            cols_ref, rows_ref = refs[n : n + 2]
            total = weight(cols_ref, rows_ref.at[:, columns], weighs) * total
        put(outs[0].at[i] if len(outs[0].shape) == 3 else outs[0], total)


def turn_kernel(a_ref, s_ref, own_ref, send_ref, s_out):
    core, _ = core_and_chip()
    rows = a_ref.shape[1]
    for i in range(own_ref.shape[0] // rows):
        for of, out in ((core, own_ref), (1 - core, send_ref)):
            columns = pl.ds(pl.multiple_of((2 * i + of) * rows, rows), rows)
            out[i * rows : (i + 1) * rows, :] = a_ref[0, :, columns].T
    s_out[...] = s_ref[0].T


def weight(cols_ref, rows_ref, j):
    return cols_ref[:, j : j + 1] * rows_ref[j : j + 1, :]


def weighed(places, cols_ref, rows_ref, messages, value):
    for j, message in zip(places, messages):
        value = value + weight(cols_ref, rows_ref, j) * get(message)
    return value


def step_kernel(into_value, into_total, more, columns, *refs):
    n = len(into_value)
    value_ref, total_ref, cols_ref, rows_ref = refs[:4]
    rows_ref = rows_ref.at[:, columns]
    messages, outs = refs[4 : 4 + n], refs[4 + n :]
    outs[0][...] = weighed(into_value, cols_ref, rows_ref, messages, value_ref[...])
    total = weight(cols_ref, rows_ref, into_total[0]) * total_ref[...]
    total = weighed(into_total[1:], cols_ref, rows_ref, messages, total)
    put(outs[1], total)
    if more:
        outs[2][...] = total


def cross_kernel(places, columns, of, value_ref, total_ref, cols_ref, rows_ref, message_ref, value_out, sent_ref):
    into_value, mix_own, mix_got = places
    at = rows_ref.at[:, columns]
    got = get(message_ref)
    value_out[...] = value_ref[:, of] + weight(cols_ref, at, into_value) * got
    put(sent_ref, weight(cols_ref, at, mix_own) * total_ref[:, of] + weight(cols_ref, at, mix_got) * got)


def side_s_kernel(places, columns, value_ref, s_ref, cols_ref, rows_ref, *refs):
    rows_ref = rows_ref.at[:, columns]
    upper = weighed(places, cols_ref, rows_ref, refs[: len(places)], value_ref[...])
    refs[-1][...] = jnp.dot(s_ref[...], upper.astype(BF16), preferred_element_type=F32).astype(BF16)


def stack_kernel(*refs):
    for i, ref in enumerate(refs[:-1]):
        refs[-1][i] = ref[...]


def side_a_kernel(picks, has_before, *refs):
    refs = list(refs)
    a_ref, (_, chip) = refs.pop(0), core_and_chip()
    solved = refs.pop(0)[...] if has_before else None
    rows = a_ref.shape[1]
    operands, features = [], []
    for array, block, part, o in picks:
        operands.append(refs[array][...] if block is None else refs[array][block])
        lanes = operands[-1].shape[1]
        start = (chip ^ o) * rows + part * lanes
        features.append(a_ref[pl.ds(pl.multiple_of(start, lanes), lanes), :])
    term = jnp.dot(jnp.concatenate(operands, axis=1), jnp.concatenate(features, axis=0), preferred_element_type=F32)
    solved = term if solved is None else solved + term
    if refs[-1].dtype == F32:
        refs[-1][...] = solved
    else:
        put(refs[-1], solved)


def joint_kernel(total_at, sent_at, own_ref, theirs_ref, cols_ref, rows_ref, value_ref, total_ref, *sent_refs):
    value = own_ref[...] + get(theirs_ref)
    value_ref[...] = value
    total_ref[...] = weight(cols_ref, rows_ref, total_at) * value
    for i, sent in enumerate(sent_refs):
        lanes = sent.shape[1]
        columns = slice(i * lanes, (i + 1) * lanes)
        total = total_ref[:, columns]
        if sent_at[i] is not None:
            total = weight(cols_ref, rows_ref.at[:, columns], sent_at[i]) * total
        put(sent, total)


def last_kernel(places, cols_ref, rows_ref, *refs):
    out_ref, turned_ref, sems = refs[-3:]
    copies = []
    for i, place in enumerate(places):
        value_ref, message_ref = refs[2 * i : 2 * i + 2]
        lanes = value_ref.shape[1]
        columns = slice(i * lanes, (i + 1) * lanes)
        lower = weighed([place], cols_ref, rows_ref.at[:, columns], [message_ref], value_ref[...])
        turned_ref[columns, :] = lower.astype(BF16).T
        rows = pl.ds(i * lanes, lanes)
        copies.append(pltpu.make_async_copy(turned_ref.at[rows], out_ref.at[0, rows], sems.at[i]))
        copies[-1].start()
    for copy in copies:
        copy.wait()


def digits(layers):
    step, out = 1, []
    while step < layers:
        size = min(4, layers // step)
        out.append((step, size))
        step *= size
    return out


def weights_kernel(step, size, last, n, *refs):
    groups, state = refs[:n], refs[n : n + (2 if step > 1 else 0)]
    cols_ref, rows_ref, *state_ref = refs[n + len(state) :]
    group = [ref[i : i + 1, :] for ref in groups for i in range(ref.shape[0])]
    ones, zeros = jnp.ones_like(group[0]), jnp.zeros_like(group[0])
    below, above = [ref[...] for ref in state] or [group[0], ones]
    mine = lax.rem(lax.div(lax.axis_index("layer"), step), size)

    def product(holds):
        out = ones
        for flip, vector in enumerate(group):
            out = out * jnp.where(holds(me ^ flip), vector, ones)
        return out

    def pick(*cases):
        out = zeros
        for at, vector in cases:
            out = jnp.where(me == at, vector, out)
        return out

    stack = [group[0]]
    for me, factor in ((mine, below), (size - 1 - mine, above)):
        if not last:
            for flip in range(1, size):
                peer = me ^ flip
                between = product(lambda q: (q > me) & (q < peer))
                stack.append(jnp.where(peer > me, factor * between, zeros))
            for flip in range(size):
                stack.append(product(lambda q: q < me ^ flip))
        elif size == 4:
            rates, beside = group[:2]
            far = factor * beside
            stack.append(pick((0, factor), (2, factor)))
            stack.append(pick((2, ones), (3, beside)))
            stack.append(pick((2, rates), (3, ones)))
            stack.append(pick((0, far), (1, factor)))
            stack.append(pick((0, far), (1, factor)))
            stack.append(pick((1, ones), (3, ones)))
            stack.append(pick((0, ones), (1, rates)))
            stack.append(pick((0, factor), (1, factor), (2, factor)))
            stack.append(pick((0, ones), (1, ones), (2, ones), (3, beside)))
        else:
            stack.append(pick((0, factor)))
    width = cols_ref.shape[0]
    stack += [zeros] * (cols_ref.shape[1] - len(stack))
    table = jnp.concatenate(stack, axis=0)
    cols_ref[...] = table[:, :width].T
    rows_ref[...] = table[: rows_ref.shape[0], width:]
    if not last:
        me = mine
        below, above = below * product(lambda q: q > me), above * product(lambda q: q < me)
        state_ref[0][...] = jnp.concatenate([product(lambda q: q >= 0), below, above], axis=0)


def weight_places(size, last):
    out = []
    for i in range(2):
        if not last:
            n = 2 * size - 1
            out.append((list(range(1 + i * n, i * n + size)), list(range(i * n + size, 1 + i * n + n))))
        elif size == 4:
            b = 1 + 9 * i
            out.append(([((1, 2), None, (b, b + 1, b + 2), b + 3), ((2, 1), b + 8, (b + 4, b + 5, b + 6), b + 7)], None))
        else:
            out.append((None, 1 + i))
    return out


def shards(activations, out_grads, a_inverse, s_inverse, in_decay, out_decay):
    layers, peers = lax.axis_size("layer"), lax.axis_size("dp")
    chips = peers // 2
    rows = a_inverse.shape[1]
    width = out_grads.shape[2]
    tokens = activations.shape[1]
    split = SPLIT if rows % (128 * SPLIT) == 0 else 1
    lanes = rows // split

    def shape(*dims, dtype=F32):
        return jax.ShapeDtypeStruct(dims, dtype)

    def message(n):
        return shape(width + TAIL, n, dtype=BF16)

    def call(kernel, out_shape, *operands, grant=4 * 2**20, hbm=0, scratch=(), after=(), anywhere=False):
        several = isinstance(out_shape, (list, tuple))
        if after:
            inner, count = kernel, len(operands)

            def kernel(*refs):
                inner(*refs[:count], *refs[count + len(after) :])

        return pl.pallas_call(
            kernel,
            out_shape=out_shape,
            in_specs=[HBM] * hbm
            + [VMEM] * (len(operands) - hbm)
            + [pl.BlockSpec(memory_space=pl.ANY)] * len(after),
            out_specs=[VMEM] * len(out_shape) if several else pl.BlockSpec(memory_space=pl.ANY) if anywhere else VMEM,
            scratch_shapes=scratch,
            compiler_params=pltpu.CompilerParams(vmem_limit_bytes=grant),
            cost_estimate=pl.CostEstimate(flops=12 * 10**8, bytes_accessed=10**8, transcendentals=0),
        )(*operands, *after)

    odd, even = list(range(1, chips, 2)), list(range(0, chips, 2))
    sent, turned, rest, inputs, rates = call(
        first_kernel,
        [
            shape(len(odd), width + TAIL, rows, dtype=BF16),
            shape(width, tokens, dtype=BF16),
            shape(len(even), tokens, rows, dtype=BF16),
            shape(chips, tokens, rows, dtype=BF16),
            shape(1, width + rows),
        ],
        *(pltpu.with_memory_space_constraint(x, pltpu.HBM) for x in (out_grads, activations, out_decay, in_decay)),
        hbm=4,
        grant=FIRST_GRANT * 2**20,
        scratch=[
            pltpu.VMEM((tokens, width), BF16),
            pltpu.VMEM((len(odd), tokens, rows), BF16),
            pltpu.SemaphoreType.DMA((2 * chips + 3,)),
        ],
    )
    theirs = {1: exchange(sent, "dp", 1)}
    outs = [shape(len(even), width + TAIL, rows, dtype=BF16), shape(width, tokens, dtype=BF16)]
    sent, turned = call(rest_kernel, outs, turned, rest, after=(sent,))
    theirs[0] = exchange(sent, "dp", 1)

    levels = [1 << b for b in range(chips.bit_length() - 1)]
    received = [{} for _ in range(split)]
    latest = []

    def blocks(part, offsets, outs, weighs=None, weights=(), passed=()):
        heard = [[(got, j) for got, j in received[part].get(o, [])] for o in offsets]
        arrays = list({id(got): got for some in heard for got, _ in some}.values())
        picks = [[([id(x) for x in arrays].index(id(got)), j) for got, j in some] for some in heard]
        outs = call(
            functools.partial(sum_kernel, part, offsets, picks, len(arrays), weighs, len(passed)),
            outs,
            turned,
            inputs,
            theirs[offsets[0] % 2],
            *arrays,
            *(weights if weighs else ()),
            *passed,
            after=latest[-1:],
        )
        latest.append(outs[0])
        return outs

    held = []
    for i, level in enumerate(levels):
        offsets = list(range(level, chips, 2 * level))
        soon, held_next = (offsets, []) if level == levels[-1] else (offsets[1:], offsets[:1])
        for part in range(split):
            for at, some in [(level, soon)] + held:
                outs = [shape(len(some), width + TAIL, lanes, dtype=BF16)]
                final = len(latest) + 1 == split * (2 * len(levels) - 1)
                sent, *passed = blocks(part, some, outs + [shape(1, width + rows)] * final, passed=[rates] * final)
                rates = passed[0] if final else rates
                got = exchange(sent, "dp", 2 * at)
                received[part].update({o ^ at: received[part].get(o ^ at, []) + [(got, j)] for j, o in enumerate(some)})
        held = [(level, held_next)] if held_next else []

    group = [rates, exchange(rates, "layer", 1)]
    ups, downs = [], []
    state = []
    for step, size in digits(layers):
        last = step * size == layers
        if step > 1:
            group = [own, exchange(own, "layer", step)]
        if size == 4 and not last:
            group = [jnp.concatenate(group, axis=0)]
            group.append(exchange(group[0], "layer", 2 * step))
        cols, in_rows, *new = call(
            functools.partial(weights_kernel, step, size, last, len(group)),
            [shape(width, 128), shape(24, rows)] + [shape(3, width + rows)] * (not last),
            *group,
            *state,
            after=latest[-1:],
        )
        if not last:
            own, state = new[0][:1], [new[0][1:2], new[0][2:]]
        for solve, places in zip((ups, downs), weight_places(size, last)):
            solve.append((step, size, cols, in_rows, *places))
    a_own, a_theirs, s_turned = call(
        turn_kernel,
        [shape(chips * rows, rows, dtype=BF16)] * 2 + [shape(width, width, dtype=BF16)],
        a_inverse,
        s_inverse,
        after=latest[-1:],
    )
    a_theirs = exchange(a_theirs, "dp", 1)

    def steps(solve, value, total, sent, part=0):
        n = value.shape[1]
        for i, (step, size, cols, in_rows, into_value, into_total) in enumerate(solve[:-1]):
            more = i + 1 < len(solve)
            outs = [shape(width, n), message(n)] + [shape(width, n)] * more
            kernel = functools.partial(step_kernel, into_value, into_total, more, pl.ds(part * n, n))
            others = [exchange(sent, "layer", flip * step) for flip in range(1, size)]
            value, sent, *total = call(kernel, outs, value, total, cols, in_rows, *others)
            total = total[0] if more else value
        return value, total, sent

    def order_of(solve, part):
        step, size, _, _, orders, place = solve[-1]
        if orders is None:
            return (step,), None, None, place
        (first, second), *places = orders[part % len(orders)]
        return (first * step, second * step), *places

    def cross(solve, part, value, total, sent):
        _, _, cols, in_rows, *_ = solve[-1]
        flips, _, places, _ = order_of(solve, part)
        n = sent.shape[1]
        got = exchange(sent, "layer", flips[0])
        if len(flips) == 1:
            return value, got
        columns = slice(part * n, (part + 1) * n)
        of = columns if value.shape[1] > n else slice(0, n)
        kernel = functools.partial(cross_kernel, places, columns, of)
        value, sent = call(kernel, [shape(width, n), message(n)], value, total, cols, in_rows, got)
        return value, exchange(sent, "layer", flips[1])

    _, _, cols, in_rows, *_ = ups[-1]
    applied = []
    for part in range(split):
        first = order_of(ups, part)[1] if len(ups) == 1 else None
        sent, value = blocks(part, [0], [message(lanes), shape(width, lanes)], first, (cols, in_rows))
        value, total, sent = steps(ups, value, value, sent, part)
        value, got = cross(ups, part, value, total, sent)
        kernel = functools.partial(side_s_kernel, [order_of(ups, part)[3]], slice(part * lanes, (part + 1) * lanes))
        applied.append(
            call(kernel, shape(width, lanes, dtype=BF16), value, s_turned, cols, in_rows, got, after=applied[-1:])
        )

    def stack(items, after=()):
        return call(stack_kernel, shape(len(items), width, lanes, dtype=BF16), *items, after=after)

    have = [{0: (rows_of, None)} for rows_of in applied]
    arrivals = [[(part, 0) for part in range(split)]]

    def send(level, batch, after=()):
        items = [have[part][o] for part, o in batch]
        if len(items) == 1 and not after:
            got = exchange(items[0][0], "dp", 2 * level)
        else:
            got = exchange(stack([x if i is None else x[i] for x, i in items], after), "dp", 2 * level)
        came = [(part, o ^ level) for part, o in batch]
        have_of = [(got, i if len(batch) > 1 or after else None) for i in range(len(batch))]
        for (part, o), where in zip(came, have_of):
            have[part][o] = where
        return came, got

    for part in range(split):
        for level in reversed(levels[1:]):
            arrivals[0] += send(level, [(part, o) for o in list(have[part])])[0]
    if chips > 1:
        plan = [[(part, 0)] for part in range(split)]
        plan += [[(part, o) for o in have[part] if o > 1] for part in range(split)]
        plan = [batch for batch in plan if batch]
        gots = []
        for i, batch in enumerate(plan):
            came, got = send(1, batch, gots[:1] if i == split else [])
            gots.append(got)
            if i + 1 < len(plan) and i:
                arrivals[-1] += came
            else:
                arrivals.append(came)

    own, others, done = None, None, []
    for chosen in arrivals:
        arrays = list({id(have[part][o][0]): have[part][o][0] for part, o in chosen}.values())
        picks = [([id(x) for x in arrays].index(id(have[part][o][0])), have[part][o][1], part, o) for part, o in chosen]

        def product(a, before, out_shape, after=()):
            before = [] if before is None else [before]
            kernel = functools.partial(side_a_kernel, picks, bool(before))
            return call(kernel, out_shape, a, *before, *arrays, after=after)

        final = chosen is arrivals[-1]
        others = product(a_theirs, others, message(rows) if final else shape(width, rows), done)
        own = product(a_own, own, shape(width, rows))
        done = [own]
    others = exchange(others, "dp", 1)

    pieces = split if len(downs) == 1 and downs[-1][1] == 4 else 1
    outs = [shape(width, rows)] * 2 + [message(rows // pieces)] * pieces
    first = [order_of(downs, part)[1] if len(downs) == 1 else None for part in range(pieces)]
    _, _, cols, in_rows, *_ = downs[0]
    value, total, *sent = call(functools.partial(joint_kernel, 0, first), outs, own, others, cols, in_rows)
    if len(downs) > 1:
        value, total, sent[0] = steps(downs, value, total, sent[0])
    operands = [x for part in range(pieces) for x in cross(downs, part, value, total, sent[part])]
    _, _, cols, in_rows, *_ = downs[-1]
    places = [order_of(downs, part)[3] for part in range(pieces)]
    return call(
        functools.partial(last_kernel, places),
        shape(1, rows, width, dtype=BF16),
        cols,
        in_rows,
        *operands,
        scratch=[pltpu.VMEM((rows, width), BF16), pltpu.SemaphoreType.DMA((len(places),))],
        anywhere=True,
    )


def solution(mesh):
    placed = (
        P("layer", "dp", None),
        P("layer", "dp", None),
        P("layer", "dp", None),
        P("layer", None, None),
        P("layer", "dp"),
        P("layer", None),
    )
    return jax.shard_map(
        shards, mesh=mesh, in_specs=placed, out_specs=P("layer", "dp", None), check_vma=False
    )
```

```python
import functools

import jax
import jax.numpy as jnp
from jax import lax
from jax.experimental import pallas as pl
from jax.experimental.pallas import tpu as pltpu
from jax.sharding import PartitionSpec as P

TAIL = 16
LIFT = 2.0**15
TINY = 1e-30
F32, BF16 = jnp.float32, jnp.bfloat16
VMEM = pl.BlockSpec(memory_space=pltpu.VMEM)
HBM = pl.BlockSpec(memory_space=pltpu.HBM)
FIRST_GRANT = 8
SPLIT = 2


def exchange(x, axis, flip):
    return lax.ppermute(x, axis, [(i, i ^ flip) for i in range(lax.axis_size(axis))])


def put(ref, value):
    rows = value.shape[0]
    top = jnp.maximum(jnp.max(jnp.abs(value), axis=0, keepdims=True), TINY).astype(BF16).astype(F32)
    ref[rows:, :] = jnp.broadcast_to(top, (TAIL, value.shape[1])).astype(BF16)
    z = value * (LIFT / top)
    z2 = z * z
    z4 = z2 * z2
    z8 = z4 * z4
    ref[:rows, :] = jnp.where(z < 0, -z8, z8).astype(BF16)


def get(ref):
    rows = ref.shape[0] - TAIL
    top = ref[rows:, :][:1, :].astype(F32) * (1.0 / LIFT)
    y = ref[:rows, :].astype(F32)
    square = lax.rsqrt(lax.rsqrt(jnp.abs(y) + 1e-37))
    size = square * lax.rsqrt(square)
    return jnp.where(y < 0, -top, top) * size


def core_and_chip():
    place = lax.axis_index("dp")
    return lax.rem(place, 2), lax.div(place, 2)


def first_kernel(
    grads_hbm, inputs_hbm, out_decay, in_decay, sent_ref, turned_ref, rest_ref, own_ref, rates_ref, *scratch
):
    grads_ref, inputs_ref, sems = scratch
    core, chip = core_and_chip()
    width = out_decay.shape[1]
    chips, _, rows = own_ref.shape
    sem = iter(range(sems.shape[0]))

    def copy(source, into):
        out = pltpu.make_async_copy(source, into, sems.at[next(sem)])
        out.start()
        return out

    def load(o, of, into):
        start = pl.multiple_of((2 * (chip ^ o) + of) * rows, rows)
        return copy(inputs_hbm.at[0, :, pl.ds(start, rows)], into)

    lead = copy(grads_hbm.at[0], grads_ref)
    theirs = [load(o, 1 - core, inputs_ref.at[i]) for i, o in enumerate(range(1, chips, 2))]
    lead.wait()
    others = [load(o, 1 - core, rest_ref.at[i]) for i, o in enumerate(range(0, chips, 2))]
    others += [load(o, core, own_ref.at[o]) for o in range(chips)]
    others.append(copy(out_decay, rates_ref.at[:, pl.ds(0, width)]))
    others.append(copy(in_decay, rates_ref.at[:, pl.ds(width, rows)]))
    turned_ref[...] = grads_ref[...].T
    for i, arrival in enumerate(theirs):
        arrival.wait()
        put(sent_ref.at[i], jnp.dot(turned_ref[...], inputs_ref[i], preferred_element_type=F32))
    for arrival in others:
        arrival.wait()


def rest_kernel(turned_ref, inputs_ref, sent_ref, turned_out):
    turned_out[...] = turned_ref[...]
    for i in range(inputs_ref.shape[0]):
        put(sent_ref.at[i], jnp.dot(turned_ref[...], inputs_ref[i], preferred_element_type=F32))


def sum_kernel(part, offsets, picks, n, weighs, passes, turned_ref, own_ref, theirs_ref, *refs):
    messages, outs = refs[:n], refs[n + (2 if weighs else 0) + passes :]
    lanes = outs[0].shape[-1]
    columns = pl.ds(part * lanes, lanes)
    if passes:
        outs[1][...] = refs[n][...]
        outs = outs[:1]
    for i, o in enumerate(offsets):
        total = jnp.dot(turned_ref[...], own_ref[o, :, columns], preferred_element_type=F32)
        total = total + get(theirs_ref.at[o // 2, :, columns])
        for array, j in picks[i]:
            total = total + get(messages[array].at[j])
        if len(outs) > 1:
            outs[1][...] = total
        if weighs:
            cols_ref, rows_ref = refs[n : n + 2]
            total = weight(cols_ref, rows_ref.at[:, columns], weighs) * total
        put(outs[0].at[i] if len(outs[0].shape) == 3 else outs[0], total)


def turn_kernel(a_ref, s_ref, own_ref, send_ref, s_out):
    core, _ = core_and_chip()
    rows = a_ref.shape[1]
    for i in range(own_ref.shape[0] // rows):
        for of, out in ((core, own_ref), (1 - core, send_ref)):
            columns = pl.ds(pl.multiple_of((2 * i + of) * rows, rows), rows)
            out[i * rows : (i + 1) * rows, :] = a_ref[0, :, columns].T
    s_out[...] = s_ref[0].T


def weight(cols_ref, rows_ref, j):
    return cols_ref[:, j : j + 1] * rows_ref[j : j + 1, :]


def weighed(places, cols_ref, rows_ref, messages, value):
    for j, message in zip(places, messages):
        value = value + weight(cols_ref, rows_ref, j) * get(message)
    return value


def step_kernel(into_value, into_total, more, columns, *refs):
    n = len(into_value)
    value_ref, total_ref, cols_ref, rows_ref = refs[:4]
    rows_ref = rows_ref.at[:, columns]
    messages, outs = refs[4 : 4 + n], refs[4 + n :]
    outs[0][...] = weighed(into_value, cols_ref, rows_ref, messages, value_ref[...])
    total = weight(cols_ref, rows_ref, into_total[0]) * total_ref[...]
    total = weighed(into_total[1:], cols_ref, rows_ref, messages, total)
    put(outs[1], total)
    if more:
        outs[2][...] = total


def cross_kernel(places, columns, of, value_ref, total_ref, cols_ref, rows_ref, message_ref, value_out, sent_ref):
    into_value, mix_own, mix_got = places
    at = rows_ref.at[:, columns]
    got = get(message_ref)
    value_out[...] = value_ref[:, of] + weight(cols_ref, at, into_value) * got
    put(sent_ref, weight(cols_ref, at, mix_own) * total_ref[:, of] + weight(cols_ref, at, mix_got) * got)


def side_s_kernel(places, columns, value_ref, s_ref, cols_ref, rows_ref, *refs):
    rows_ref = rows_ref.at[:, columns]
    upper = weighed(places, cols_ref, rows_ref, refs[: len(places)], value_ref[...])
    refs[-1][...] = jnp.dot(s_ref[...], upper.astype(BF16), preferred_element_type=F32).astype(BF16)


def stack_kernel(*refs):
    for i, ref in enumerate(refs[:-1]):
        refs[-1][i] = ref[...]


def side_a_kernel(picks, has_before, *refs):
    refs = list(refs)
    a_ref, (_, chip) = refs.pop(0), core_and_chip()
    solved = refs.pop(0)[...] if has_before else None
    rows = a_ref.shape[1]
    operands, features = [], []
    for array, block, part, o in picks:
        operands.append(refs[array][...] if block is None else refs[array][block])
        lanes = operands[-1].shape[1]
        start = (chip ^ o) * rows + part * lanes
        features.append(a_ref[pl.ds(pl.multiple_of(start, lanes), lanes), :])
    term = jnp.dot(jnp.concatenate(operands, axis=1), jnp.concatenate(features, axis=0), preferred_element_type=F32)
    solved = term if solved is None else solved + term
    if refs[-1].dtype == F32:
        refs[-1][...] = solved
    else:
        put(refs[-1], solved)


def joint_kernel(total_at, sent_at, own_ref, theirs_ref, cols_ref, rows_ref, value_ref, total_ref, *sent_refs):
    value = own_ref[...] + get(theirs_ref)
    value_ref[...] = value
    total_ref[...] = weight(cols_ref, rows_ref, total_at) * value
    for i, sent in enumerate(sent_refs):
        lanes = sent.shape[1]
        columns = slice(i * lanes, (i + 1) * lanes)
        total = total_ref[:, columns]
        if sent_at[i] is not None:
            total = weight(cols_ref, rows_ref.at[:, columns], sent_at[i]) * total
        put(sent, total)


def last_kernel(places, cols_ref, rows_ref, *refs):
    out_ref, turned_ref, sems = refs[-3:]
    copies = []
    for i, place in enumerate(places):
        value_ref, message_ref = refs[2 * i : 2 * i + 2]
        lanes = value_ref.shape[1]
        columns = slice(i * lanes, (i + 1) * lanes)
        lower = weighed([place], cols_ref, rows_ref.at[:, columns], [message_ref], value_ref[...])
        turned_ref[columns, :] = lower.astype(BF16).T
        rows = pl.ds(i * lanes, lanes)
        copies.append(pltpu.make_async_copy(turned_ref.at[rows], out_ref.at[0, rows], sems.at[i]))
        copies[-1].start()
    for copy in copies:
        copy.wait()


def digits(layers):
    step, out = 1, []
    while step < layers:
        size = min(4, layers // step)
        out.append((step, size))
        step *= size
    return out


def weights_kernel(step, size, last, n, *refs):
    groups, state = refs[:n], refs[n : n + (2 if step > 1 else 0)]
    cols_ref, rows_ref, *state_ref = refs[n + len(state) :]
    group = [ref[i : i + 1, :] for ref in groups for i in range(ref.shape[0])]
    ones, zeros = jnp.ones_like(group[0]), jnp.zeros_like(group[0])
    below, above = [ref[...] for ref in state] or [group[0], ones]
    mine = lax.rem(lax.div(lax.axis_index("layer"), step), size)

    def product(holds):
        out = ones
        for flip, vector in enumerate(group):
            out = out * jnp.where(holds(me ^ flip), vector, ones)
        return out

    def pick(*cases):
        out = zeros
        for at, vector in cases:
            out = jnp.where(me == at, vector, out)
        return out

    stack = [group[0]]
    for me, factor in ((mine, below), (size - 1 - mine, above)):
        if not last:
            for flip in range(1, size):
                peer = me ^ flip
                between = product(lambda q: (q > me) & (q < peer))
                stack.append(jnp.where(peer > me, factor * between, zeros))
            for flip in range(size):
                stack.append(product(lambda q: q < me ^ flip))
        elif size == 4:
            rates, beside = group[:2]
            far = factor * beside
            stack.append(pick((0, factor), (2, factor)))
            stack.append(pick((2, ones), (3, beside)))
            stack.append(pick((2, rates), (3, ones)))
            stack.append(pick((0, far), (1, factor)))
            stack.append(pick((0, far), (1, factor)))
            stack.append(pick((1, ones), (3, ones)))
            stack.append(pick((0, ones), (1, rates)))
            stack.append(pick((0, factor), (1, factor), (2, factor)))
            stack.append(pick((0, ones), (1, ones), (2, ones), (3, beside)))
        else:
            stack.append(pick((0, factor)))
    width = cols_ref.shape[0]
    stack += [zeros] * (cols_ref.shape[1] - len(stack))
    table = jnp.concatenate(stack, axis=0)
    cols_ref[...] = table[:, :width].T
    rows_ref[...] = table[: rows_ref.shape[0], width:]
    if not last:
        me = mine
        below, above = below * product(lambda q: q > me), above * product(lambda q: q < me)
        state_ref[0][...] = jnp.concatenate([product(lambda q: q >= 0), below, above], axis=0)


def weight_places(size, last):
    out = []
    for i in range(2):
        if not last:
            n = 2 * size - 1
            out.append((list(range(1 + i * n, i * n + size)), list(range(i * n + size, 1 + i * n + n))))
        elif size == 4:
            b = 1 + 9 * i
            out.append(([((1, 2), None, (b, b + 1, b + 2), b + 3), ((2, 1), b + 8, (b + 4, b + 5, b + 6), b + 7)], None))
        else:
            out.append((None, 1 + i))
    return out


def shards(activations, out_grads, a_inverse, s_inverse, in_decay, out_decay):
    layers, peers = lax.axis_size("layer"), lax.axis_size("dp")
    chips = peers // 2
    rows = a_inverse.shape[1]
    width = out_grads.shape[2]
    tokens = activations.shape[1]
    split = SPLIT if rows % (128 * SPLIT) == 0 else 1
    lanes = rows // split

    def shape(*dims, dtype=F32):
        return jax.ShapeDtypeStruct(dims, dtype)

    def message(n):
        return shape(width + TAIL, n, dtype=BF16)

    def call(kernel, out_shape, *operands, grant=4 * 2**20, hbm=0, scratch=(), after=(), anywhere=False):
        several = isinstance(out_shape, (list, tuple))
        if after:
            inner, count = kernel, len(operands)

            def kernel(*refs):
                inner(*refs[:count], *refs[count + len(after) :])

        return pl.pallas_call(
            kernel,
            out_shape=out_shape,
            in_specs=[HBM] * hbm
            + [VMEM] * (len(operands) - hbm)
            + [pl.BlockSpec(memory_space=pl.ANY)] * len(after),
            out_specs=[VMEM] * len(out_shape) if several else pl.BlockSpec(memory_space=pl.ANY) if anywhere else VMEM,
            scratch_shapes=scratch,
            compiler_params=pltpu.CompilerParams(vmem_limit_bytes=grant),
            cost_estimate=pl.CostEstimate(flops=12 * 10**8, bytes_accessed=10**8, transcendentals=0),
        )(*operands, *after)

    odd, even = list(range(1, chips, 2)), list(range(0, chips, 2))
    sent, turned, rest, inputs, rates = call(
        first_kernel,
        [
            shape(len(odd), width + TAIL, rows, dtype=BF16),
            shape(width, tokens, dtype=BF16),
            shape(len(even), tokens, rows, dtype=BF16),
            shape(chips, tokens, rows, dtype=BF16),
            shape(1, width + rows),
        ],
        *(pltpu.with_memory_space_constraint(x, pltpu.HBM) for x in (out_grads, activations, out_decay, in_decay)),
        hbm=4,
        grant=FIRST_GRANT * 2**20,
        scratch=[
            pltpu.VMEM((tokens, width), BF16),
            pltpu.VMEM((len(odd), tokens, rows), BF16),
            pltpu.SemaphoreType.DMA((2 * chips + 3,)),
        ],
    )
    theirs = {1: exchange(sent, "dp", 1)}
    outs = [shape(len(even), width + TAIL, rows, dtype=BF16), shape(width, tokens, dtype=BF16)]
    sent, turned = call(rest_kernel, outs, turned, rest, after=(sent,))
    theirs[0] = exchange(sent, "dp", 1)

    levels = [1 << b for b in range(chips.bit_length() - 1)]
    received = [{} for _ in range(split)]
    latest = []

    def blocks(part, offsets, outs, weighs=None, weights=(), passed=()):
        heard = [[(got, j) for got, j in received[part].get(o, [])] for o in offsets]
        arrays = list({id(got): got for some in heard for got, _ in some}.values())
        picks = [[([id(x) for x in arrays].index(id(got)), j) for got, j in some] for some in heard]
        outs = call(
            functools.partial(sum_kernel, part, offsets, picks, len(arrays), weighs, len(passed)),
            outs,
            turned,
            inputs,
            theirs[offsets[0] % 2],
            *arrays,
            *(weights if weighs else ()),
            *passed,
            after=latest[-1:],
        )
        latest.append(outs[0])
        return outs

    held = []
    for i, level in enumerate(levels):
        offsets = list(range(level, chips, 2 * level))
        soon, held_next = (offsets, []) if level == levels[-1] else (offsets[1:], offsets[:1])
        for part in range(split):
            for at, some in [(level, soon)] + held:
                outs = [shape(len(some), width + TAIL, lanes, dtype=BF16)]
                final = len(latest) + 1 == split * (2 * len(levels) - 1)
                sent, *passed = blocks(part, some, outs + [shape(1, width + rows)] * final, passed=[rates] * final)
                rates = passed[0] if final else rates
                got = exchange(sent, "dp", 2 * at)
                received[part].update({o ^ at: received[part].get(o ^ at, []) + [(got, j)] for j, o in enumerate(some)})
        held = [(level, held_next)] if held_next else []

    group = [rates, exchange(rates, "layer", 1)]
    ups, downs = [], []
    state = []
    for step, size in digits(layers):
        last = step * size == layers
        if step > 1:
            group = [own, exchange(own, "layer", step)]
        if size == 4 and not last:
            group = [jnp.concatenate(group, axis=0)]
            group.append(exchange(group[0], "layer", 2 * step))
        cols, in_rows, *new = call(
            functools.partial(weights_kernel, step, size, last, len(group)),
            [shape(width, 128), shape(24, rows)] + [shape(3, width + rows)] * (not last),
            *group,
            *state,
            after=latest[-1:],
        )
        if not last:
            own, state = new[0][:1], [new[0][1:2], new[0][2:]]
        for solve, places in zip((ups, downs), weight_places(size, last)):
            solve.append((step, size, cols, in_rows, *places))
    a_own, a_theirs, s_turned = call(
        turn_kernel,
        [shape(chips * rows, rows, dtype=BF16)] * 2 + [shape(width, width, dtype=BF16)],
        a_inverse,
        s_inverse,
        after=latest[-1:],
    )
    a_theirs = exchange(a_theirs, "dp", 1)

    def steps(solve, value, total, sent, part=0):
        n = value.shape[1]
        for i, (step, size, cols, in_rows, into_value, into_total) in enumerate(solve[:-1]):
            more = i + 1 < len(solve)
            outs = [shape(width, n), message(n)] + [shape(width, n)] * more
            kernel = functools.partial(step_kernel, into_value, into_total, more, pl.ds(part * n, n))
            others = [exchange(sent, "layer", flip * step) for flip in range(1, size)]
            value, sent, *total = call(kernel, outs, value, total, cols, in_rows, *others)
            total = total[0] if more else value
        return value, total, sent

    def order_of(solve, part):
        step, size, _, _, orders, place = solve[-1]
        if orders is None:
            return (step,), None, None, place
        (first, second), *places = orders[part % len(orders)]
        return (first * step, second * step), *places

    def cross(solve, part, value, total, sent):
        _, _, cols, in_rows, *_ = solve[-1]
        flips, _, places, _ = order_of(solve, part)
        n = sent.shape[1]
        got = exchange(sent, "layer", flips[0])
        if len(flips) == 1:
            return value, got
        columns = slice(part * n, (part + 1) * n)
        of = columns if value.shape[1] > n else slice(0, n)
        kernel = functools.partial(cross_kernel, places, columns, of)
        value, sent = call(kernel, [shape(width, n), message(n)], value, total, cols, in_rows, got)
        return value, exchange(sent, "layer", flips[1])

    _, _, cols, in_rows, *_ = ups[-1]
    applied = []
    for part in range(split):
        first = order_of(ups, part)[1] if len(ups) == 1 else None
        sent, value = blocks(part, [0], [message(lanes), shape(width, lanes)], first, (cols, in_rows))
        value, total, sent = steps(ups, value, value, sent, part)
        value, got = cross(ups, part, value, total, sent)
        kernel = functools.partial(side_s_kernel, [order_of(ups, part)[3]], slice(part * lanes, (part + 1) * lanes))
        applied.append(
            call(kernel, shape(width, lanes, dtype=BF16), value, s_turned, cols, in_rows, got, after=applied[-1:])
        )

    def stack(items, after=()):
        return call(stack_kernel, shape(len(items), width, lanes, dtype=BF16), *items, after=after)

    have = [{0: (rows_of, None)} for rows_of in applied]
    arrivals = [[(part, 0) for part in range(split)]]

    def send(level, batch, after=()):
        items = [have[part][o] for part, o in batch]
        if len(items) == 1 and not after:
            got = exchange(items[0][0], "dp", 2 * level)
        else:
            got = exchange(stack([x if i is None else x[i] for x, i in items], after), "dp", 2 * level)
        came = [(part, o ^ level) for part, o in batch]
        have_of = [(got, i if len(batch) > 1 or after else None) for i in range(len(batch))]
        for (part, o), where in zip(came, have_of):
            have[part][o] = where
        return came, got

    for part in range(split):
        for level in reversed(levels[1:]):
            arrivals[0] += send(level, [(part, o) for o in list(have[part])])[0]
    if chips > 1:
        plan = [[(part, 0)] for part in range(split)]
        plan += [[(part, o) for o in have[part] if o > 1] for part in range(split)]
        plan = [batch for batch in plan if batch]
        gots = []
        for i, batch in enumerate(plan):
            came, got = send(1, batch, gots[:1] if i == split else [])
            gots.append(got)
            if i + 1 < len(plan) and i:
                arrivals[-1] += came
            else:
                arrivals.append(came)

    own, others, done = None, None, []
    for chosen in arrivals:
        arrays = list({id(have[part][o][0]): have[part][o][0] for part, o in chosen}.values())
        picks = [([id(x) for x in arrays].index(id(have[part][o][0])), have[part][o][1], part, o) for part, o in chosen]

        def product(a, before, out_shape, after=()):
            before = [] if before is None else [before]
            kernel = functools.partial(side_a_kernel, picks, bool(before))
            return call(kernel, out_shape, a, *before, *arrays, after=after)

        final = chosen is arrivals[-1]
        others = product(a_theirs, others, message(rows) if final else shape(width, rows), done)
        own = product(a_own, own, shape(width, rows))
        done = [own]
    others = exchange(others, "dp", 1)

    pieces = split if len(downs) == 1 and downs[-1][1] == 4 else 1
    outs = [shape(width, rows)] * 2 + [message(rows // pieces)] * pieces
    first = [order_of(downs, part)[1] if len(downs) == 1 else None for part in range(pieces)]
    _, _, cols, in_rows, *_ = downs[0]
    value, total, *sent = call(functools.partial(joint_kernel, 0, first), outs, own, others, cols, in_rows)
    if len(downs) > 1:
        value, total, sent[0] = steps(downs, value, total, sent[0])
    operands = [x for part in range(pieces) for x in cross(downs, part, value, total, sent[part])]
    _, _, cols, in_rows, *_ = downs[-1]
    places = [order_of(downs, part)[3] for part in range(pieces)]
    return call(
        functools.partial(last_kernel, places),
        shape(1, rows, width, dtype=BF16),
        cols,
        in_rows,
        *operands,
        scratch=[pltpu.VMEM((rows, width), BF16), pltpu.SemaphoreType.DMA((len(places),))],
        anywhere=True,
    )


def solution(mesh):
    placed = (
        P("layer", "dp", None),
        P("layer", "dp", None),
        P("layer", "dp", None),
        P("layer", None, None),
        P("layer", "dp"),
        P("layer", None),
    )
    return jax.shard_map(
        shards, mesh=mesh, in_specs=placed, out_specs=P("layer", "dp", None), check_vma=False
    )
```
